32 devices in a mesh: rows: 8 (over z, x), proto: 4 (over y, core).
Axes of the slice: x: 2, y: 2, z: 4, core: 2. Of those that a mesh axis runs over, the one named last changes fastest.
Arguments:
- teacher_features: bfloat16 [256, 256], P('rows'), may hold values from -6 to 6
- student_features: bfloat16 [1280, 256], P('rows'), may hold values from -8 to 8
- prototypes: bfloat16 [256, 131072], P(None, 'proto'), may hold values from -1 to 1
- pairing: int32 [1280], P('rows'), may hold values from 0 to 255
Outputs:
- proto_grad: float32 [256, 131072], P('rows', 'proto')
- student_grad: float32 [1280, 256], P('rows', 'proto')
- loss: float32 [1280], P('rows')
The draws below stay inside these ranges and needn't reach their ends.
All inputs are finite; a program needn't handle non-finite values.
Results may differ from the reference program's by a relative error of at most 0.0023.
Values may be sent and summed in bfloat16 or wider, within the bound.
No kernel may reach another device: no remote copies, remote signals or barrier semaphores. Data moves between devices by JAX's collectives and lax.ppermute only.
A program may use at most 192 MiB of HBM per device.

```python
import jax
import jax.numpy as jnp
from jax import lax

D = 256
K = 131072
ITERS = 3
S_DEV = 160
TEACH_ROWS = 256
STUD_ROWS = 1280
N_ROWS = 8


def shared_direction(key):
    signs = jax.random.randint(jax.random.fold_in(key, 77), (D,), 0, 2).astype(jnp.float32)
    return (2.0 * signs - 1.0) * D ** (-0.5)


def draw_prototypes(key, part):
    direction = shared_direction(key)
    key = jax.random.fold_in(key, 11)
    position = (jnp.arange(K, dtype=jnp.float32) + 0.5) / K
    noise = jax.random.truncated_normal(key, -4.0, 4.0, (D, K), jnp.float32)
    slope = 0.5
    values = noise * D ** (-0.5) + (slope * position)[None, :] * direction[:, None]
    return values.astype(jnp.bfloat16)


def draw_student_features(key, part):
    direction = shared_direction(key)
    key = jax.random.fold_in(key, 23)
    noise_key, weight_key = jax.random.split(key)
    noise = jax.random.truncated_normal(noise_key, -5.0, 5.0, (STUD_ROWS, D), jnp.float32)
    along = jax.random.uniform(weight_key, (STUD_ROWS,), jnp.float32, 0.5, 1.5)
    values = noise + (along * D ** 0.5)[:, None] * direction[None, :]
    return values.astype(jnp.bfloat16)


def set_ends(entries, stream_key, low, top_value):
    longest = entries.shape.index(max(entries.shape))
    spots = []
    for shift in (0, 1):
        where = [jax.random.randint(jax.random.fold_in(stream_key, axis), (), 0, length) for axis, length in enumerate(entries.shape)]
        where[longest] = (where[longest] + shift) % entries.shape[longest]
        spots.append(tuple(where))
    return entries.at[spots[0]].set(low).at[spots[1]].set(top_value)


def block_levels(rng, extent, cuts, low, largest):
    def one(axis_at, parts):
        steps = jax.random.uniform(jax.random.fold_in(jax.random.fold_in(rng, 6), axis_at), (parts,), jnp.float32, low / len(cuts), largest / len(cuts))
        return jnp.repeat(jnp.exp(steps), extent[axis_at] // parts).reshape((-1,) + (1,) * (len(extent) - axis_at - 1))

    gain = one(*cuts[0])
    for cut in cuts[1:]:
        gain = gain * one(*cut)
    return gain


def centred(rng, shape, spread, reach, pieces=(), kind=jnp.bfloat16):
    result = spread * jax.random.normal(rng, shape, jnp.float32)
    if pieces:
        result = result * block_levels(rng, shape, pieces, -0.22, 0.18)
    return jnp.clip(result, -reach, reach).astype(kind)


def setup_inputs(seed: int = 0) -> dict:
    arg_keys = jax.random.split(jax.random.key(seed), 5)
    teacher_features = centred(arg_keys[0], (TEACH_ROWS, D), 1.0, 6.0, ((0, 8),))
    student_features = draw_student_features(jax.random.fold_in(arg_keys[4], 71), 0)
    prototypes = draw_prototypes(jax.random.fold_in(arg_keys[4], 71), 0)
    pairing = set_ends(jax.random.randint(arg_keys[3], (STUD_ROWS,), 0, TEACH_ROWS), jax.random.fold_in(arg_keys[3], 1), 0, TEACH_ROWS - 1).astype(jnp.int32)
    return {"teacher_features": teacher_features, "student_features": student_features, "prototypes": prototypes, "pairing": pairing}


teacher_temp = 0.07
student_temp = 0.1
eps = 1e-06

def reference(teacher_features, student_features, prototypes, pairing):
    vf = prototypes.astype(jnp.float32)
    vnorm = jnp.sqrt(lax.optimization_barrier(jnp.sum(vf * vf, axis=0)) + eps)
    unit = vf / vnorm[None, :]
    unit_b = unit.astype(jnp.bfloat16)
    tf = teacher_features.astype(jnp.float32)
    teach_unit = (tf / jnp.sqrt(lax.optimization_barrier(jnp.sum(tf * tf, axis=1, keepdims=True)) + eps)).astype(jnp.bfloat16)
    energy = jnp.exp(jnp.dot(teach_unit, unit_b, preferred_element_type=jnp.float32) / teacher_temp)
    row_scale = jnp.ones((TEACH_ROWS,), jnp.float32)
    col_scale = jnp.ones((K,), jnp.float32)
    for step in range(ITERS):
        col_sum = col_scale * lax.optimization_barrier(jnp.sum(energy * row_scale[:, None], axis=0))
        col_scale = col_scale / (col_sum * K)
        row_sum = row_scale * lax.optimization_barrier(jnp.sum(energy * col_scale[None, :], axis=1))
        row_scale = row_scale / (row_sum * TEACH_ROWS)
    teach_target = (energy * col_scale[None, :] * row_scale[:, None] * TEACH_ROWS).astype(jnp.bfloat16)
    grad_scale = K / 64.0
    blocks = student_features.reshape(N_ROWS, S_DEV, D)
    block_pairs = pairing.reshape(N_ROWS, S_DEV)

    def one_block(head, item):
        feats, pairs = item
        sf = feats.astype(jnp.float32)
        snorm = jnp.sqrt(lax.optimization_barrier(jnp.sum(sf * sf, axis=1, keepdims=True)) + eps)
        stud_unit = sf / snorm
        stud_unit_b = stud_unit.astype(jnp.bfloat16)
        target = jnp.take(teach_target, pairs.astype(jnp.int32), axis=0).astype(jnp.float32)
        logits = jnp.dot(stud_unit_b, unit_b, preferred_element_type=jnp.float32) / student_temp
        expo = jnp.exp(logits)
        denom = lax.optimization_barrier(jnp.sum(expo, axis=1))
        cross = lax.optimization_barrier(jnp.sum(target * logits, axis=1))
        mass = lax.optimization_barrier(jnp.sum(target, axis=1))
        loss = jnp.log(denom) * mass - cross
        dlogit = (grad_scale / student_temp * (mass[:, None] * (expo / denom[:, None]) - target)).astype(jnp.bfloat16)
        head = head + jnp.dot(stud_unit_b.T, dlogit, preferred_element_type=jnp.float32)
        back = jnp.dot(dlogit, unit_b.T, preferred_element_type=jnp.float32)
        along = lax.optimization_barrier(jnp.sum(stud_unit * back, axis=1, keepdims=True))
        grad = (back - stud_unit * along) / snorm
        return (head, (grad, loss))
    head, (grads, losses) = lax.scan(one_block, jnp.zeros((D, K), jnp.float32), (blocks, block_pairs))
    proj = lax.optimization_barrier(jnp.sum(unit * head, axis=0))
    proto_grad = (head - unit * proj[None, :]) / vnorm[None, :]
    return (proto_grad, grads.reshape(STUD_ROWS, D), losses.reshape(STUD_ROWS))
```

```python
import functools

import jax
import jax.numpy as jnp
from jax import lax
from jax.experimental import pallas as pl
from jax.experimental.pallas import tpu as pltpu
from jax.sharding import PartitionSpec as P

teacher_temp = 0.07
student_temp = 0.1
eps = 1e-06
LOG2E = 1.4426950408889634
GROUP = 4
F32 = jnp.float32
BF16 = jnp.bfloat16
NT = (((1,), (1,)), ((), ()))


def params(mib):
    return pltpu.CompilerParams(vmem_limit_bytes=mib * 1024 * 1024)


def whole(shape):
    return pl.BlockSpec(shape, lambda i, *_: (0,) * len(shape))


def cols(rows, width):
    return pl.BlockSpec((rows, width), lambda i, *_: (0, i))


def to_column(row):
    return jnp.broadcast_to(row, (128, row.shape[1])).T


def lane_sums(x):
    total = x[:, :128]
    for at in range(128, x.shape[1], 128):
        total = total + x[:, at : at + 128]
    return total


def to_row(acc):
    return jnp.sum(acc.T, axis=0, keepdims=True)


def unit_kernel(place, v_ref, unit_ref, inv_ref):
    v = v_ref[...].astype(F32)
    inv = lax.rsqrt(jnp.sum(v * v, axis=0, keepdims=True) + eps)
    unit_ref[...] = (v * inv).astype(BF16)
    inv_ref[...] = inv


def unit_call(place, v, kl, width):
    d = v.shape[0]
    steps = kl // width
    return pl.pallas_call(
        unit_kernel,
        out_shape=(jax.ShapeDtypeStruct((d, kl), BF16), jax.ShapeDtypeStruct((1, kl), F32)),
        grid_spec=pltpu.PrefetchScalarGridSpec(
            num_scalar_prefetch=1,
            grid=(steps,),
            in_specs=[pl.BlockSpec((d, width), lambda i, p: (0, p[0] * steps + i))],
            out_specs=(cols(d, width), cols(1, width)),
        ),
        cost_estimate=pl.CostEstimate(flops=4 * d * kl, bytes_accessed=4 * d * kl, transcendentals=kl),
        compiler_params=params(32),
        name="unit",
    )(place, v)


def energy_kernel(total_k, teach_ref, unit_ref, energy_ref, sum_ref, acc):
    i = pl.program_id(0)
    dots = jnp.dot(teach_ref[...], unit_ref[...], preferred_element_type=F32)
    energy = jnp.exp2(dots * (LOG2E / teacher_temp))
    energy_ref[...] = energy
    col = 1.0 / (jnp.sum(energy, axis=0, keepdims=True) * total_k)
    part = lane_sums(energy * col)

    @pl.when(i == 0)
    def _():
        acc[...] = part

    @pl.when(i > 0)
    def _():
        acc[...] += part

    @pl.when(i == pl.num_programs(0) - 1)
    def _():
        sum_ref[...] = to_row(acc[...])


def energy_call(teach, unit_b, total_k, width):
    t, d = teach.shape
    kl = unit_b.shape[1]
    return pl.pallas_call(
        functools.partial(energy_kernel, float(total_k)),
        out_shape=(jax.ShapeDtypeStruct((t, kl), F32), jax.ShapeDtypeStruct((1, t), F32)),
        grid=(kl // width,),
        in_specs=[whole((t, d)), cols(d, width)],
        out_specs=(cols(t, width), whole((1, t))),
        scratch_shapes=[pltpu.VMEM((t, 128), F32)],
        cost_estimate=pl.CostEstimate(
            flops=2 * t * d * kl, bytes_accessed=4 * t * kl + 2 * d * kl, transcendentals=t * kl
        ),
        compiler_params=params(32),
        name="energy",
    )(teach, unit_b)


def iterate_kernel(total_k, last, sum_in, energy_ref, *refs):
    if last:
        unit_ref, sum_ref, scaled_ref, mean_ref, acc, row = refs
    else:
        sum_ref, acc, row = refs
    i = pl.program_id(0)
    t, width = energy_ref.shape

    @pl.when(i == 0)
    def _():
        row[...] = to_column(1.0 / (sum_in[...] * float(t)))

    scale = row[...]
    mass = []
    for at in range(0, width, 128):
        mass.append(jnp.sum(energy_ref[:, at : at + 128] * scale, axis=0, keepdims=True))
    part = None
    for n, at in enumerate(range(0, width, 128)):
        scaled = energy_ref[:, at : at + 128] * (1.0 / (mass[n] * total_k))
        if last:
            scaled_ref[:, at : at + 128] = scaled.astype(BF16)
        part = scaled if part is None else part + scaled

    @pl.when(i == 0)
    def _():
        acc[...] = part

    @pl.when(i > 0)
    def _():
        acc[...] += part

    if last:
        mean = lax.dot_general(unit_ref[...], scaled_ref[...], NT, preferred_element_type=F32)

        @pl.when(i == 0)
        def _():
            mean_ref[...] = mean

        @pl.when(i > 0)
        def _():
            mean_ref[...] += mean

    @pl.when(i == pl.num_programs(0) - 1)
    def _():
        sum_ref[...] = to_row(acc[...])


def iterate_call(sums, energy, unit_b, total_k, width, last):
    t, kl = energy.shape
    d = unit_b.shape[0]
    out_shape = [jax.ShapeDtypeStruct((1, t), F32)]
    out_specs = [whole((1, t))]
    in_specs = [whole((1, t)), cols(t, width)]
    args = [sums, energy]
    if last:
        out_shape += [jax.ShapeDtypeStruct((t, kl), BF16), jax.ShapeDtypeStruct((d, t), F32)]
        out_specs += [cols(t, width), whole((d, t))]
        in_specs += [cols(d, width)]
        args += [unit_b]
    return pl.pallas_call(
        functools.partial(iterate_kernel, float(total_k), last),
        out_shape=out_shape,
        grid=(kl // width,),
        in_specs=in_specs,
        out_specs=out_specs,
        scratch_shapes=[pltpu.VMEM((t, 128), F32), pltpu.VMEM((t, 128), F32)],
        cost_estimate=pl.CostEstimate(flops=4 * t * kl, bytes_accessed=4 * t * kl, transcendentals=kl),
        compiler_params=params(32),
        name="iterate_last" if last else "iterate",
    )(*args)


def student_kernel(block, place, stud_ref, unit_ref, expo_ref, denom_ref, pull_ref, acc):
    i = pl.program_id(0)
    s = stud_ref.shape[0]

    @pl.when(i == 0)
    def _():
        acc[...] = jnp.zeros_like(acc)
        pull_ref[...] = jnp.zeros_like(pull_ref)

    for at in range(0, s, block):
        logits = jnp.dot(stud_ref[at : at + block, :], unit_ref[...], preferred_element_type=F32)
        expo = jnp.exp2(logits * (LOG2E / student_temp))
        expo_ref[at : at + block, :] = expo.astype(BF16)
        acc[at : at + block, :] += lane_sums(expo)
    mine = pull_ref.shape[1]
    start = pl.multiple_of(place[1] * mine, 128)
    pull_ref[...] += lax.dot_general(
        unit_ref[...], expo_ref[pl.ds(start, mine), :], NT, preferred_element_type=F32
    )

    @pl.when(i == pl.num_programs(0) - 1)
    def _():
        denom_ref[...] = to_row(acc[...])


def student_call(place, stud, unit_b, mine, width):
    s, d = stud.shape
    kl = unit_b.shape[1]
    return pl.pallas_call(
        functools.partial(student_kernel, 256),
        out_shape=(
            jax.ShapeDtypeStruct((s, kl), BF16),
            jax.ShapeDtypeStruct((1, s), F32),
            jax.ShapeDtypeStruct((d, mine), F32),
        ),
        grid_spec=pltpu.PrefetchScalarGridSpec(
            num_scalar_prefetch=1,
            grid=(kl // width,),
            in_specs=[whole((s, d)), cols(d, width)],
            out_specs=(cols(s, width), whole((1, s)), whole((d, mine))),
            scratch_shapes=[pltpu.VMEM((s, 128), F32)],
        ),
        cost_estimate=pl.CostEstimate(
            flops=2 * (s + mine) * d * kl, bytes_accessed=2 * (s + d) * kl, transcendentals=s * kl
        ),
        compiler_params=params(48),
        name="student",
    )(place, stud, unit_b)


def pick(column, pairs):
    t, n = column.shape[0], pairs.shape[1]
    which = lax.broadcasted_iota(jnp.int32, (t, 128), 0)
    out = []
    for at in range(0, n, 128):
        hit = which == pairs[:, at : at + 128]
        out.append(jnp.sum(jnp.where(hit, column, 0.0), axis=0, keepdims=True))
    return jnp.concatenate(out, axis=1)


def gather_kernel(stud_ref, pairs_ref, stud_t_ref, weight_ref):
    t = weight_ref.shape[1]
    s = stud_ref.shape[0]
    stud_t = stud_ref[...].astype(F32).T.astype(BF16)
    stud_t_ref[...] = stud_t
    which = lax.broadcasted_iota(jnp.int32, (t, s), 0)
    onehot = (which == pairs_ref[...]).astype(F32).astype(BF16)
    weight_ref[...] = lax.dot_general(stud_t, onehot, NT, preferred_element_type=F32)


def gather_call(stud, pairs, t):
    s, d = stud.shape
    return pl.pallas_call(
        gather_kernel,
        out_shape=(jax.ShapeDtypeStruct((d, s), BF16), jax.ShapeDtypeStruct((d, t), F32)),
        cost_estimate=pl.CostEstimate(flops=2 * s * d * t, bytes_accessed=6 * s * d, transcendentals=0),
        compiler_params=params(48),
        name="by_teacher",
    )(stud, pairs)


def head_kernel(factor, place, sums_ref, denom_ref, pairs_ref, stud_t_ref, weight_ref, expo_ref,
                scaled_ref, v_ref, inv_ref, own_ref, *refs):
    sends, (lhs, lhs_teach, grad) = refs[:-3], refs[-3:]
    t = scaled_ref.shape[0]

    @pl.when(pl.program_id(0) == 0)
    def _():
        sums = sums_ref[...]
        row = 1.0 / (sums * float(t))
        mass = pick(to_column(row * sums * float(t)), pairs_ref[...])
        lhs[...] = (stud_t_ref[...].astype(F32) * (mass / denom_ref[...] * factor)).astype(BF16)
        lhs_teach[...] = (weight_ref[...] * (row * (-factor * t))).astype(BF16)

    head = jnp.dot(lhs[...], expo_ref[...], preferred_element_type=F32)
    head = head + jnp.dot(lhs_teach[...], scaled_ref[...], preferred_element_type=F32)
    inv = inv_ref[...]
    unit = v_ref[...].astype(F32) * inv
    proj = jnp.sum(unit * head, axis=0, keepdims=True)
    grad[...] = (head - unit * proj) * inv
    rows = own_ref.shape[0]
    base = place[1] * (rows * GROUP)

    def part(n):
        start = pl.multiple_of(base + (place[0] ^ n) * rows, rows)
        return grad[pl.ds(start, rows), :]

    own_ref[...] = part(0)
    for n, ref in enumerate(sends):
        ref[...] = part(n + 1).astype(BF16)


def head_call(place, sums, denom, pairs, stud_t, weight, expo, scaled, v, inv, factor, rows, width):
    d, s = stud_t.shape
    t = scaled.shape[0]
    kl = expo.shape[1]
    steps = kl // width
    return pl.pallas_call(
        functools.partial(head_kernel, factor),
        out_shape=[jax.ShapeDtypeStruct((rows, v.shape[1]), F32)]
        + [jax.ShapeDtypeStruct((rows, kl), BF16)] * (GROUP - 1),
        grid_spec=pltpu.PrefetchScalarGridSpec(
            num_scalar_prefetch=1,
            grid=(steps,),
            in_specs=[
                whole((1, t)), whole((1, s)), whole((1, s)), whole((d, s)), whole((d, t)),
                cols(s, width), cols(t, width),
                pl.BlockSpec((d, width), lambda i, p: (0, p[0] * steps + i)),
                cols(1, width),
            ],
            out_specs=[pl.BlockSpec((rows, width), lambda i, p: (0, p[0] * steps + i))]
            + [cols(rows, width)] * (GROUP - 1),
            scratch_shapes=[pltpu.VMEM((d, s), BF16), pltpu.VMEM((d, t), BF16), pltpu.VMEM((d, width), F32)],
        ),
        cost_estimate=pl.CostEstimate(
            flops=2 * (s + t) * d * kl, bytes_accessed=2 * (s + t + d) * kl, transcendentals=0
        ),
        compiler_params=params(48),
        name="head",
    )(place, sums, denom, pairs, stud_t, weight, expo, scaled, v, inv)


def back_kernel(factor, sums_ref, denom_ref, pairs_ref, stud_t_ref, pull_ref, mean_ref, back_ref):
    d, n = pull_ref.shape
    t = mean_ref.shape[1]
    sums = sums_ref[...]
    row = 1.0 / (sums * float(t))
    pairs = pairs_ref[...]
    mass = pick(to_column(row * sums * float(t)), pairs)
    which = lax.broadcasted_iota(jnp.int32, (t, n), 0)
    onehot = (which == pairs).astype(F32)
    target = jnp.dot(
        mean_ref[...] * (row * t), onehot, preferred_element_type=F32, precision=lax.Precision.HIGHEST
    )
    stud_t = stud_t_ref[...].astype(F32)
    back = (pull_ref[...] * (mass / denom_ref[...]) - target) * factor
    back_ref[:d, :] = back
    along = jnp.sum(stud_t * back, axis=0, keepdims=True)
    cross = jnp.sum(stud_t * target, axis=0, keepdims=True) * (1.0 / student_temp)
    at = lax.broadcasted_iota(jnp.int32, (8, n), 0)
    back_ref[d:, :] = jnp.where(at == 0, along, jnp.where(at == 1, cross, 0.0))


def back_call(sums, denom, pairs, stud_t, pull, mean, factor):
    d, n = pull.shape
    return pl.pallas_call(
        functools.partial(back_kernel, factor),
        out_shape=jax.ShapeDtypeStruct((d + 8, n), F32),
        cost_estimate=pl.CostEstimate(flops=12 * d * n * mean.shape[1], bytes_accessed=12 * d * n, transcendentals=0),
        compiler_params=params(48),
        name="back",
    )(sums, denom, pairs, stud_t, pull, mean)


def body(teacher_features, student_features, v, pairing):
    n_rows, n_proto = lax.axis_size("rows"), lax.axis_size("proto")
    r, p = lax.axis_index("rows"), lax.axis_index("proto")
    d, local_k = v.shape
    total_k = local_k * n_proto
    kl = local_k // GROUP
    t_dev, s_dev = teacher_features.shape[0], student_features.shape[0]
    t, s = t_dev * n_rows, s_dev * n_rows
    at, group = r % GROUP, r // GROUP
    place = jnp.stack([at, group]).astype(jnp.int32)
    factor = total_k / 64.0 / student_temp

    def swap_rows(x, n):
        return lax.ppermute(x, "rows", [(j, j ^ n) for j in range(n_rows)])

    def swap_proto(x, n):
        return lax.ppermute(x, "proto", [(j, j ^ n) for j in range(n_proto)])

    def total(x):
        n = 1
        while n < n_proto:
            x = x + swap_proto(x, n)
            n *= 2
        n = 1
        while n < GROUP:
            x = x + swap_rows(x, n)
            n *= 2
        return x

    tf = teacher_features.astype(F32)
    teach = (tf / jnp.sqrt(jnp.sum(tf * tf, axis=1, keepdims=True) + eps)).astype(BF16)
    sf = student_features.astype(F32)
    snorm = jnp.sqrt(jnp.sum(sf * sf, axis=1, keepdims=True) + eps)
    stud_unit = sf / snorm
    stud = stud_unit.astype(BF16)

    lines = 16 * -(-(-(-s_dev // d)) // 8)
    half = lines // 2
    flat = jnp.pad(pairing, (0, half * d - s_dev)).reshape(half, d)
    digits = jnp.concatenate([flat // 64, flat % 64], axis=0).astype(BF16)

    def join(x, n):
        other = swap_rows(x, n)
        low = (r // n) % 2 == 0
        return jnp.concatenate([jnp.where(low, x, other), jnp.where(low, other, x)], axis=0)

    packed = jnp.concatenate([teach, stud, digits], axis=0)[None]
    n = 1
    while n < GROUP:
        packed = join(packed, n)
        n *= 2
    teach_all, rest = packed[:, :t_dev], packed[:, t_dev:]
    while n < n_rows:
        teach_all = join(teach_all, n)
        rest = join(rest, n)
        n *= 2
    teach_all = teach_all.reshape(t, d)
    stud_all = rest[:, :s_dev].reshape(s, d)
    digits = rest[:, s_dev:].astype(jnp.int32)
    digits = digits[:, :half] * 64 + digits[:, half:]
    pairs = digits.reshape(n_rows, half * d)[:, :s_dev].reshape(1, s)

    width = min(1024, kl)
    unit_b, inv = unit_call(place, v, kl, width)
    energy, sums = energy_call(teach_all, unit_b, total_k, width)
    mine = s_dev * GROUP
    expo, denom, pull = student_call(place, stud_all, unit_b, mine, min(512, kl))
    stud_t, weight = gather_call(stud_all, pairs, t)
    (sums,) = iterate_call(total(sums), energy, unit_b, total_k, width, False)
    sums, scaled, mean = iterate_call(total(sums), energy, unit_b, total_k, width, True)
    both = total(jnp.concatenate([sums, denom], axis=1))
    sums, denom = both[:, :t], both[:, t:]

    rows = d // n_rows
    grads = head_call(
        place, sums, denom, pairs, stud_t, weight, expo, scaled, v, inv, factor, rows, min(1024, kl)
    )
    proto_grad = grads[0]
    for n in range(1, GROUP):
        got = swap_rows(grads[n], n).astype(F32)
        proto_grad = lax.dynamic_update_slice(proto_grad, got, (0, (at ^ n) * kl))

    def of_group(x):
        return lax.dynamic_slice_in_dim(x, group * mine, mine, 1)

    back = back_call(sums, of_group(denom), of_group(pairs), of_group(stud_t), pull, mean, factor)
    body_rows, tail = back[:d], back[d:]
    n = n_proto // 2
    while n >= 1:
        height = body_rows.shape[0] // 2
        bit = (p // n) % 2
        keep = lax.dynamic_slice_in_dim(body_rows, bit * height, height, 0)
        send = lax.dynamic_slice_in_dim(body_rows, (1 - bit) * height, height, 0)
        got = swap_proto(jnp.concatenate([send, tail], axis=0), n)
        body_rows, tail = keep + got[:height], tail + got[height:]
        n //= 2
    terms = jnp.concatenate([body_rows, tail], axis=0)

    def block(n):
        return lax.dynamic_slice_in_dim(terms, (at ^ n) * s_dev, s_dev, 1)

    full = block(0)
    for n in range(1, GROUP):
        full = full + swap_rows(block(n), n)
    share = d // n_proto
    along, cross = full[share], full[share + 1]
    stud_part = lax.dynamic_slice_in_dim(stud_unit, p * share, share, 1)
    student_grad = (full[:share].T - stud_part * along[:, None]) / snorm
    own = lax.dynamic_slice_in_dim(denom[0], r * s_dev, s_dev, 0)
    own_pairs = pairing
    row = 1.0 / (sums[0] * t)
    mass = jnp.take(row * sums[0] * t, own_pairs, axis=0)
    loss = jnp.log(own) * mass - cross
    return (proto_grad, student_grad, loss)


def solution(mesh):
    return jax.shard_map(
        body,
        mesh=mesh,
        in_specs=(P("rows", None), P("rows", None), P(None, "proto"), P("rows")),
        out_specs=(P("rows", "proto"), P("rows", "proto"), P("rows")),
        check_vma=False,
    )
```

```python
import functools

import jax
import jax.numpy as jnp
from jax import lax
from jax.experimental import pallas as pl
from jax.experimental.pallas import tpu as pltpu
from jax.sharding import PartitionSpec as P

teacher_temp = 0.07
student_temp = 0.1
eps = 1e-06
LOG2E = 1.4426950408889634
GROUP = 4
CHUNKS = 8
LIMIT = 58
F32 = jnp.float32
BF16 = jnp.bfloat16
NT = (((1,), (1,)), ((), ()))


def params(mib):
    return pltpu.CompilerParams(vmem_limit_bytes=mib * 1024 * 1024)


def vmem(count):
    return [pl.BlockSpec(memory_space=pltpu.VMEM)] * count


def anywhere(count):
    return [pl.BlockSpec(memory_space=pl.ANY)] * count


def grid_one(*shapes):
    return [pl.BlockSpec(shape, lambda i, n=len(shape): (0,) * n) for shape in shapes]


SMEM = pl.BlockSpec(memory_space=pltpu.SMEM)
DMA = pltpu.SemaphoreType.DMA
AHEAD = 3


def begin(chunks, fetch):
    for i in range(min(AHEAD, chunks)):
        for copy in fetch(i):
            copy.start()


def stream(chunks, fetch, work):
    @pl.loop(0, chunks)
    def _(i):
        @pl.when(i + AHEAD < chunks)
        def _():
            for copy in fetch(i + AHEAD):
                copy.start()

        for copy in fetch(i):
            copy.wait()
        work(i)


def to_column(row):
    return jnp.broadcast_to(row, (128, row.shape[1])).T


def lane_sums(x):
    total = x[:, :128]
    for at in range(128, x.shape[1], 128):
        total = total + x[:, at : at + 128]
    return total


def to_row(acc):
    return jnp.sum(acc.T, axis=0, keepdims=True)


def pick(column, pairs):
    t, n = column.shape[0], pairs.shape[1]
    out = []
    for at in range(0, n, 128):
        width = min(128, n - at)
        which = lax.broadcasted_iota(jnp.int32, (t, width), 0)
        hit = which == pairs[:, at : at + width]
        out.append(jnp.sum(jnp.where(hit, column[:, :width], 0.0), axis=0, keepdims=True))
    return jnp.concatenate(out, axis=1)


def prepare_kernel(teach_ref, stud_ref, pairs_ref, out_ref, digits):
    t, s = teach_ref.shape[0], stud_ref.shape[0]
    for ref, at, n in ((teach_ref, 0, t), (stud_ref, t, s)):
        x = ref[...].astype(F32)
        norm = jnp.sqrt(jnp.sum(x * x, axis=1, keepdims=True) + eps)
        out_ref[at : at + n, :] = (x / norm).astype(BF16)
    pairs = pairs_ref[...]
    high = lax.shift_right_logical(pairs, 6)
    row = lax.broadcasted_iota(jnp.int32, (16, s), 0)
    digits[...] = jnp.zeros_like(digits)
    digits[:, :s] = jnp.where(row == 0, high, jnp.where(row == 1, pairs - high * 64, 0)).astype(F32)
    out_ref[t + s :, :] = digits[...].astype(BF16)


def prepare_call(teach, stud, pairs):
    t, s, d = teach.shape[0], stud.shape[0], stud.shape[1]
    return pl.pallas_call(
        prepare_kernel,
        out_shape=jax.ShapeDtypeStruct((t + s + 16, d), BF16),
        grid=(1,),
        in_specs=grid_one((t, d), (s, d), (1, s)),
        out_specs=grid_one((t + s + 16, d))[0],
        scratch_shapes=[pltpu.VMEM((16, d), F32)],
        compiler_params=params(LIMIT),
        name="prepare",
    )(teach, stud, pairs)


def unit_kernel(place, v_hbm, unit_hbm, inv_ref, v, unit, sems_in, sems_out):
    chunks, _, width = v.shape

    def fetch(i):
        start = pl.multiple_of((place[0] * chunks + i) * width, width)
        return (pltpu.make_async_copy(v_hbm.at[:, pl.ds(start, width)], v.at[i], sems_in.at[i]),)

    def store(i):
        return pltpu.make_async_copy(unit.at[i], unit_hbm.at[i], sems_out.at[i])

    begin(chunks, fetch)

    def work(i):
        x = v[i].astype(F32)
        inv = lax.rsqrt(jnp.sum(x * x, axis=0, keepdims=True) + eps)
        unit[i] = (x * inv).astype(BF16)
        inv_ref[i] = inv
        store(i).start()

    stream(chunks, fetch, work)
    for i in range(chunks):
        store(i).wait()


def unit_call(place, v, kl):
    d = v.shape[0]
    shape = (CHUNKS, d, kl // CHUNKS)
    return pl.pallas_call(
        unit_kernel,
        out_shape=(
            jax.ShapeDtypeStruct(shape, BF16),
            jax.ShapeDtypeStruct((CHUNKS, 1, kl // CHUNKS), F32),
        ),
        in_specs=[SMEM] + anywhere(1),
        out_specs=tuple(anywhere(1) + vmem(1)),
        scratch_shapes=[pltpu.VMEM(shape, BF16), pltpu.VMEM(shape, BF16), DMA((CHUNKS,)), DMA((CHUNKS,))],
        cost_estimate=pl.CostEstimate(flops=4 * d * kl, bytes_accessed=4 * d * kl, transcendentals=kl),
        compiler_params=params(LIMIT),
        name="unit",
    )(place, v)


def energy_kernel(total_k, teach_ref, unit_hbm, energy_hbm, sum_ref, unit, energy, acc, sems_in, sems_out):
    chunks = unit.shape[0]

    def fetch(i):
        return (pltpu.make_async_copy(unit_hbm.at[i], unit.at[i], sems_in.at[i]),)

    def store(i):
        return pltpu.make_async_copy(energy.at[i], energy_hbm.at[i], sems_out.at[i])

    begin(chunks, fetch)
    acc[...] = jnp.zeros_like(acc)

    def work(i):
        dots = jnp.dot(teach_ref[...], unit[i], preferred_element_type=F32)
        e = jnp.exp2(dots * (LOG2E / teacher_temp))
        energy[i] = e.astype(BF16)
        store(i).start()
        col = 1.0 / (jnp.sum(e, axis=0, keepdims=True) * total_k)
        acc[...] += lane_sums(e * col)

    stream(chunks, fetch, work)
    sum_ref[...] = to_row(acc[...])
    for i in range(chunks):
        store(i).wait()


def energy_call(teach, unit, total_k):
    t, d = teach.shape
    chunks, _, width = unit.shape
    shape = (chunks, t, width)
    return pl.pallas_call(
        functools.partial(energy_kernel, float(total_k)),
        out_shape=(jax.ShapeDtypeStruct(shape, BF16), jax.ShapeDtypeStruct((1, t), F32)),
        in_specs=vmem(1) + anywhere(1),
        out_specs=tuple(anywhere(1) + vmem(1)),
        scratch_shapes=[
            pltpu.VMEM(unit.shape, BF16), pltpu.VMEM(shape, BF16), pltpu.VMEM((t, 128), F32),
            DMA((chunks,)), DMA((chunks,)),
        ],
        cost_estimate=pl.CostEstimate(
            flops=2 * t * d * chunks * width, bytes_accessed=4 * t * chunks * width, transcendentals=0
        ),
        compiler_params=params(LIMIT),
        name="energy",
    )(teach, unit)


def iterate_kernel(total_k, last, sum_in, energy_hbm, *refs):
    if last:
        unit_hbm, denom_ref, sum_ref, mean_ref, scaled_hbm = refs[:5]
        acc, row, energy, sems_in, scaled, unit, sems_out = refs[5:]
        mean_ref[...] = jnp.zeros_like(mean_ref)
    else:
        sum_ref, acc, row, energy, sems_in = refs
    chunks, t, width = energy.shape

    def fetch(i):
        copy = pltpu.make_async_copy(energy_hbm.at[i], energy.at[i], sems_in.at[i, 0])
        if not last:
            return (copy,)
        return (copy, pltpu.make_async_copy(unit_hbm.at[i], unit.at[i], sems_in.at[i, 1]))

    def store(i):
        return pltpu.make_async_copy(scaled.at[i], scaled_hbm.at[i], sems_out.at[i])

    begin(chunks, fetch)
    row[...] = to_column(1.0 / (sum_in[...] * float(t)))
    acc[...] = jnp.zeros_like(acc)

    def work(i):
        scale = row[...]
        col = []
        for at in range(0, width, 128):
            mass = jnp.sum(energy[i, :, at : at + 128].astype(F32) * scale, axis=0, keepdims=True)
            col.append(1.0 / (mass * total_k))
        part = None
        for n, at in enumerate(range(0, width, 128)):
            x = energy[i, :, at : at + 128].astype(F32) * col[n]
            if last:
                scaled[i, :, at : at + 128] = x.astype(BF16)
            part = x if part is None else part + x
        acc[...] += part
        if last:
            store(i).start()
            mean_ref[...] += lax.dot_general(unit[i], scaled[i], NT, preferred_element_type=F32)

    stream(chunks, fetch, work)
    sum_ref[:, :t] = to_row(acc[...])
    if last:
        sum_ref[:, t:] = denom_ref[...]
        for i in range(chunks):
            store(i).wait()


def iterate_call(sums, energy, total_k, more=()):
    chunks, t, width = energy.shape
    last = bool(more)
    out_shape = [jax.ShapeDtypeStruct((1, t), F32)]
    in_specs, out_specs = vmem(1) + anywhere(1), vmem(1)
    scratch = [
        pltpu.VMEM((t, 128), F32), pltpu.VMEM((t, 128), F32), pltpu.VMEM(energy.shape, BF16), DMA((chunks, 2))
    ]
    if last:
        unit, denom = more
        d = unit.shape[1]
        out_shape = [
            jax.ShapeDtypeStruct((1, t + denom.shape[1]), F32),
            jax.ShapeDtypeStruct((d, t), F32),
            jax.ShapeDtypeStruct(energy.shape, BF16),
        ]
        in_specs, out_specs = in_specs + anywhere(1) + vmem(1), vmem(2) + anywhere(1)
        scratch += [pltpu.VMEM(energy.shape, BF16), pltpu.VMEM(unit.shape, BF16), DMA((chunks,))]
    return pl.pallas_call(
        functools.partial(iterate_kernel, float(total_k), last),
        out_shape=out_shape,
        in_specs=in_specs,
        out_specs=out_specs,
        scratch_shapes=scratch,
        cost_estimate=pl.CostEstimate(
            flops=4 * t * chunks * width, bytes_accessed=4 * t * chunks * width, transcendentals=0
        ),
        compiler_params=params(LIMIT),
        name="iterate_last" if last else "iterate",
    )(sums, energy, *more)


def student_kernel(place, rest_ref, pairs_ref, unit_hbm, expo_hbm, denom_ref, pull_ref, stud_t_hbm, weight_hbm,
                   unit, expo, acc, pull, stud, stud_t, weight, sems_in, sems_out, sems):
    chunks, s, width = expo.shape
    s_dev = s // rest_ref.shape[0]
    n = pull.shape[0]
    t = weight.shape[1]
    start = pl.multiple_of(place[1] * n, 128)

    def fetch(i):
        return (pltpu.make_async_copy(unit_hbm.at[i], unit.at[i], sems_in.at[i]),)

    def store(i):
        return pltpu.make_async_copy(expo.at[i], expo_hbm.at[i], sems_out.at[i])

    begin(chunks, fetch)
    acc[...] = jnp.zeros_like(acc)
    pull[...] = jnp.zeros_like(pull)
    for i in range(rest_ref.shape[0]):
        stud[i * s_dev : (i + 1) * s_dev, :] = rest_ref[i, :s_dev, :]
    rows_t = stud[...].astype(F32).T.astype(BF16)
    stud_t[...] = rows_t
    which = lax.broadcasted_iota(jnp.int32, (t, s), 0)
    onehot = (which == pairs_ref[...]).astype(F32).astype(BF16)
    weight[...] = lax.dot_general(rows_t, onehot, NT, preferred_element_type=F32)
    extra = (
        pltpu.make_async_copy(stud_t, stud_t_hbm, sems.at[0]),
        pltpu.make_async_copy(weight, weight_hbm, sems.at[1]),
    )
    for copy in extra:
        copy.start()

    def work(i):
        for at in range(0, s, 256):
            logits = jnp.dot(stud[at : at + 256, :], unit[i], preferred_element_type=F32)
            x = jnp.exp2(logits * (LOG2E / student_temp))
            expo[i, at : at + 256, :] = x.astype(BF16)
            acc[at : at + 256, :] += lane_sums(x)
        store(i).start()
        pull[...] += lax.dot_general(expo[i, pl.ds(start, n), :], unit[i], NT, preferred_element_type=F32)

    stream(chunks, fetch, work)
    denom_ref[...] = to_row(acc[...])
    pull_ref[...] = pull[...].T
    for copy in extra:
        copy.wait()
    for i in range(chunks):
        store(i).wait()


def student_call(place, rest, pairs, unit, t, n):
    chunks, d, width = unit.shape
    s = rest.shape[0] * (rest.shape[1] - 16)
    shape = (chunks, s, width)
    return pl.pallas_call(
        student_kernel,
        out_shape=(
            jax.ShapeDtypeStruct(shape, BF16),
            jax.ShapeDtypeStruct((1, s), F32),
            jax.ShapeDtypeStruct((d, n), F32),
            jax.ShapeDtypeStruct((d, s), BF16),
            jax.ShapeDtypeStruct((d, t), F32),
        ),
        in_specs=[SMEM] + vmem(2) + anywhere(1),
        out_specs=tuple(anywhere(1) + vmem(2) + anywhere(2)),
        scratch_shapes=[
            pltpu.VMEM(unit.shape, BF16), pltpu.VMEM(shape, BF16), pltpu.VMEM((s, 128), F32),
            pltpu.VMEM((n, d), F32), pltpu.VMEM((s, d), BF16), pltpu.VMEM((d, s), BF16), pltpu.VMEM((d, t), F32),
            DMA((chunks,)), DMA((chunks,)), DMA((2,)),
        ],
        cost_estimate=pl.CostEstimate(
            flops=4 * s * d * chunks * width, bytes_accessed=2 * s * chunks * width, transcendentals=0
        ),
        compiler_params=params(LIMIT),
        name="student",
    )(place, rest, pairs, unit)


def head_kernel(factor, place, both_ref, pairs_ref, stud_t_ref, weight_ref, inv_ref, expo_hbm,
                scaled_hbm, v_hbm, own_hbm, *refs):
    sends, refs = refs[: GROUP - 1], refs[GROUP - 1 :]
    lhs, lhs_teach, grad, expo, scaled, v, own, sems_in, sems_out = refs
    chunks, t, width = scaled.shape
    rows = own.shape[1]

    def start_of(i):
        return pl.multiple_of((place[0] * chunks + i) * width, width)

    def fetches(i):
        return (
            pltpu.make_async_copy(expo_hbm.at[i], expo.at[i], sems_in.at[i, 0]),
            pltpu.make_async_copy(scaled_hbm.at[i], scaled.at[i], sems_in.at[i, 1]),
            pltpu.make_async_copy(v_hbm.at[:, pl.ds(start_of(i), width)], v.at[i], sems_in.at[i, 2]),
        )

    def store(i):
        return pltpu.make_async_copy(own.at[i], own_hbm.at[:, pl.ds(start_of(i), width)], sems_out.at[i])

    begin(chunks, fetches)
    sums, denom = both_ref[:, :t], both_ref[:, t:]
    row = 1.0 / (sums * float(t))
    mass = pick(to_column(row * sums * float(t)), pairs_ref[...])
    lhs[...] = (stud_t_ref[...].astype(F32) * (mass / denom * factor)).astype(BF16)
    lhs_teach[...] = (weight_ref[...] * (row * (-factor * t))).astype(BF16)
    base = place[1] * (rows * GROUP)

    def part(n):
        start = pl.multiple_of(base + (place[0] ^ n) * rows, rows)
        return grad[pl.ds(start, rows), :]

    def work(i):
        head = jnp.dot(lhs[...], expo[i], preferred_element_type=F32)
        head = head + jnp.dot(lhs_teach[...], scaled[i], preferred_element_type=F32)
        inv = inv_ref[i]
        unit = v[i].astype(F32) * inv
        proj = jnp.sum(unit * head, axis=0, keepdims=True)
        grad[...] = (head - unit * proj) * inv
        own[i] = part(0)
        store(i).start()
        at = pl.ds(pl.multiple_of(i * width, width), width)
        for n, ref in enumerate(sends):
            ref[:, at] = part(n + 1).astype(BF16)

    stream(chunks, fetches, work)
    for i in range(chunks):
        store(i).wait()


def head_call(place, both, pairs, stud_t, weight, inv, expo, scaled, v, factor, rows):
    d, s = stud_t.shape
    chunks, t, width = scaled.shape
    kl = chunks * width
    return pl.pallas_call(
        functools.partial(head_kernel, factor),
        out_shape=[jax.ShapeDtypeStruct((rows, v.shape[1]), F32)]
        + [jax.ShapeDtypeStruct((rows, kl), BF16)] * (GROUP - 1),
        in_specs=[SMEM] + vmem(5) + anywhere(3),
        out_specs=anywhere(1) + vmem(GROUP - 1),
        scratch_shapes=[
            pltpu.VMEM((d, s), BF16), pltpu.VMEM((d, t), BF16), pltpu.VMEM((d, width), F32),
            pltpu.VMEM(expo.shape, BF16), pltpu.VMEM(scaled.shape, BF16), pltpu.VMEM((chunks, d, width), BF16),
            pltpu.VMEM((chunks, rows, width), F32), DMA((chunks, 3)), DMA((chunks,)),
        ],
        cost_estimate=pl.CostEstimate(
            flops=4 * (s + t) * d * kl, bytes_accessed=2 * (s + t + d) * kl, transcendentals=0
        ),
        compiler_params=params(LIMIT),
        name="head",
    )(place, both, pairs, stud_t, weight, inv, expo, scaled, v)


def back_kernel(factor, place, both_ref, pairs_ref, stud_t_ref, pull_ref, mean_ref, back_ref):
    d, n = pull_ref.shape
    t = mean_ref.shape[1]
    start = pl.multiple_of(place[1] * n, 128)
    mine = pl.ds(start, n)
    sums = both_ref[:, :t]
    denom = both_ref[:, pl.ds(pl.multiple_of(t + place[1] * n, 128), n)]
    row = 1.0 / (sums * float(t))
    pairs = pairs_ref[:, mine]
    mass = pick(to_column(row * sums * float(t)), pairs)
    which = lax.broadcasted_iota(jnp.int32, (t, n), 0)
    onehot = (which == pairs).astype(F32)
    target = jnp.dot(
        mean_ref[...] * (row * t), onehot, preferred_element_type=F32, precision=lax.Precision.HIGHEST
    )
    stud_t = stud_t_ref[:, mine].astype(F32)
    back = (pull_ref[...] * (mass / denom) - target) * factor
    back_ref[:d, :] = back
    along = jnp.sum(stud_t * back, axis=0, keepdims=True)
    cross = jnp.sum(stud_t * target, axis=0, keepdims=True) * (1.0 / student_temp)
    at = lax.broadcasted_iota(jnp.int32, (8, n), 0)
    back_ref[d:, :] = jnp.where(at == 0, along, jnp.where(at == 1, cross, 0.0))


def back_call(place, both, pairs, stud_t, pull, mean, factor):
    d, n = pull.shape
    return pl.pallas_call(
        functools.partial(back_kernel, factor),
        out_shape=jax.ShapeDtypeStruct((d + 8, n), F32),
        in_specs=[SMEM] + vmem(5),
        out_specs=vmem(1)[0],
        cost_estimate=pl.CostEstimate(flops=12 * d * n * mean.shape[1], bytes_accessed=12 * d * n, transcendentals=0),
        compiler_params=params(LIMIT),
        name="back",
    )(place, both, pairs, stud_t, pull, mean)


def finish_kernel(t, place, both_ref, denom_ref, pairs_ref, stud_ref, *refs):
    terms, (grad_ref, loss_ref, unit) = refs[:GROUP], refs[GROUP:]
    total = (terms[0][...] + terms[1][...]) + (terms[2][...] + terms[3][...])
    share = grad_ref.shape[0]
    x = stud_ref[...].astype(F32).T
    norm = jnp.sqrt(jnp.sum(x * x, axis=0, keepdims=True) + eps)
    unit[...] = x / norm
    part = unit[pl.ds(pl.multiple_of(place[2] * share, share), share), :]
    along, cross = total[share : share + 1, :], total[share + 1 : share + 2, :]
    grad_ref[...] = (total[:share, :] - part * along) / norm
    sums = both_ref[:, :t]
    mass = pick(to_column(1.0 / (sums * float(t)) * sums * float(t)), pairs_ref[...])
    loss_ref[...] = jnp.log(denom_ref[...]) * mass - cross


def finish_call(t, place, both, denom, pairs, stud, terms, share):
    s, d = stud.shape
    return pl.pallas_call(
        functools.partial(finish_kernel, t),
        out_shape=(jax.ShapeDtypeStruct((share, s), F32), jax.ShapeDtypeStruct((1, s), F32)),
        in_specs=[SMEM] + vmem(4 + GROUP),
        out_specs=tuple(vmem(2)),
        scratch_shapes=[pltpu.VMEM((d, s), F32)],
        compiler_params=params(8),
        name="finish",
    )(place, both, denom, pairs, stud, *terms)


def body(teacher_features, student_features, v, pairing):
    n_rows, n_proto = lax.axis_size("rows"), lax.axis_size("proto")
    r, p = lax.axis_index("rows"), lax.axis_index("proto")
    d, local_k = v.shape
    total_k = local_k * n_proto
    kl = local_k // GROUP
    t_dev, s_dev = teacher_features.shape[0], student_features.shape[0]
    t, s = t_dev * n_rows, s_dev * n_rows
    at, group = r % GROUP, r // GROUP
    place = jnp.stack([at, group, p]).astype(jnp.int32)
    factor = total_k / 64.0 / student_temp

    def swap_rows(x, n):
        return lax.ppermute(x, "rows", [(j, j ^ n) for j in range(n_rows)])

    def swap_proto(x, n):
        return lax.ppermute(x, "proto", [(j, j ^ n) for j in range(n_proto)])

    def total(x):
        for swap, size in ((swap_proto, n_proto), (swap_rows, GROUP)):
            n = 1
            while n < size:
                x = (x + swap(x, n)) + (swap(x, 2 * n) + swap(x, 3 * n))
                n *= 4
        return x

    def join(x, n, other=None):
        other = swap_rows(x, n) if other is None else other
        low = (r // n) % 2 == 0
        return jnp.concatenate([jnp.where(low, x, other), jnp.where(low, other, x)], axis=0)

    own_pairs = pairing.reshape(1, s_dev)
    unit, inv = unit_call(place, v, kl)
    packed = prepare_call(teacher_features, student_features, own_pairs)[None]
    packed = join(packed, 1)
    other, unit, inv = lax.optimization_barrier((swap_rows(packed, 2), unit, inv))
    packed = join(packed, 2, other)
    teach_all, rest = packed[:, :t_dev], packed[:, t_dev:]
    n = GROUP
    while n < n_rows:
        teach_all = join(teach_all, n)
        rest = join(rest, n)
        n *= 2
    teach_all = teach_all.reshape(t, d)
    digits = rest[:, s_dev : s_dev + 2, :s_dev].astype(F32)
    pairs = (digits[:, 0] * 64.0 + digits[:, 1]).astype(jnp.int32).reshape(1, s)

    energy, sums = energy_call(teach_all, unit, total_k)
    expo, denom, pull, stud_t, weight = student_call(place, rest, pairs, unit, t, s_dev * GROUP)
    (sums,) = iterate_call(total(sums), energy, total_k)
    both, mean, scaled = iterate_call(total(sums), energy, total_k, (unit, denom))
    both = total(both)

    rows = d // n_rows
    grads = head_call(place, both, pairs, stud_t, weight, inv, expo, scaled, v, factor, rows)
    proto_grad = grads[0]
    for n in range(1, GROUP):
        got = swap_rows(grads[n], n).astype(F32)
        proto_grad = lax.dynamic_update_slice(proto_grad, got, (0, (at ^ n) * kl))

    back = back_call(place, both, pairs, stud_t, pull, mean, factor)
    body_rows, tail = back[:d], back[d:]
    n = n_proto // 2
    while n >= 1:
        height = body_rows.shape[0] // 2
        bit = (p // n) % 2
        keep = lax.dynamic_slice_in_dim(body_rows, bit * height, height, 0)
        send = lax.dynamic_slice_in_dim(body_rows, (1 - bit) * height, height, 0)
        got = swap_proto(jnp.concatenate([send, tail], axis=0), n)
        body_rows, tail = keep + got[:height], tail + got[height:]
        n //= 2
    terms = jnp.concatenate([body_rows, tail], axis=0)

    def block(n):
        return lax.dynamic_slice_in_dim(terms, (at ^ n) * s_dev, s_dev, 1)

    parts = [block(0)] + [swap_rows(block(n), n) for n in range(1, GROUP)]
    own = lax.dynamic_slice_in_dim(both, t + r * s_dev, s_dev, 1)
    student_grad, loss = finish_call(t, place, both, own, own_pairs, student_features, parts, d // n_proto)
    return (proto_grad, student_grad.T, loss.reshape(s_dev))


def solution(mesh):
    return jax.shard_map(
        body,
        mesh=mesh,
        in_specs=(P("rows", None), P("rows", None), P(None, "proto"), P("rows")),
        out_specs=(P("rows", "proto"), P("rows", "proto"), P("rows")),
        check_vma=False,
    )
```

```python
import functools

import jax
import jax.numpy as jnp
from jax import lax
from jax.experimental import pallas as pl
from jax.experimental.pallas import tpu as pltpu
from jax.sharding import PartitionSpec as P

teacher_temp = 0.07
student_temp = 0.1
eps = 1e-06
LOG2E = 1.4426950408889634
GROUP = 4
CHUNKS = 8
LIMIT = 50
PARTS = 2
F32 = jnp.float32
BF16 = jnp.bfloat16
NT = (((1,), (1,)), ((), ()))


def params(mib):
    return pltpu.CompilerParams(vmem_limit_bytes=mib * 1024 * 1024)


def vmem(count):
    return [pl.BlockSpec(memory_space=pltpu.VMEM)] * count


def anywhere(count):
    return [pl.BlockSpec(memory_space=pl.ANY)] * count


def grid_one(*shapes):
    return [pl.BlockSpec(shape, lambda i, n=len(shape): (0,) * n) for shape in shapes]


SMEM = pl.BlockSpec(memory_space=pltpu.SMEM)
DMA = pltpu.SemaphoreType.DMA
AHEAD = 3


def begin(chunks, fetch):
    for i in range(min(AHEAD, chunks)):
        for copy in fetch(i):
            copy.start()


def stream(chunks, fetch, work):
    @pl.loop(0, chunks)
    def _(i):
        @pl.when(i + AHEAD < chunks)
        def _():
            for copy in fetch(i + AHEAD):
                copy.start()

        for copy in fetch(i):
            copy.wait()
        work(i)


def to_column(row):
    return jnp.broadcast_to(row, (128, row.shape[1])).T


def lane_sums(x):
    total = x[:, :128]
    for at in range(128, x.shape[1], 128):
        total = total + x[:, at : at + 128]
    return total


def to_row(acc):
    return jnp.sum(acc.T, axis=0, keepdims=True)


def pick(column, pairs):
    t, n = column.shape[0], pairs.shape[1]
    out = []
    for at in range(0, n, 128):
        width = min(128, n - at)
        which = lax.broadcasted_iota(jnp.int32, (t, width), 0)
        hit = which == pairs[:, at : at + width]
        out.append(jnp.sum(jnp.where(hit, column[:, :width], 0.0), axis=0, keepdims=True))
    return jnp.concatenate(out, axis=1)


def prepare_kernel(teach_ref, stud_ref, pairs_ref, out_ref, digits):
    t, s = teach_ref.shape[0], stud_ref.shape[0]
    for ref, at, n in ((teach_ref, 0, t), (stud_ref, t, s)):
        x = ref[...].astype(F32)
        norm = jnp.sqrt(jnp.sum(x * x, axis=1, keepdims=True) + eps)
        out_ref[at : at + n, :] = (x / norm).astype(BF16)
    pairs = pairs_ref[...]
    high = lax.shift_right_logical(pairs, 6)
    row = lax.broadcasted_iota(jnp.int32, (16, s), 0)
    digits[...] = jnp.zeros_like(digits)
    digits[:, :s] = jnp.where(row == 0, high, jnp.where(row == 1, pairs - high * 64, 0)).astype(F32)
    out_ref[t + s :, :] = digits[...].astype(BF16)


def prepare_call(teach, stud, pairs):
    t, s, d = teach.shape[0], stud.shape[0], stud.shape[1]
    return pl.pallas_call(
        prepare_kernel,
        out_shape=jax.ShapeDtypeStruct((t + s + 16, d), BF16),
        grid=(1,),
        in_specs=grid_one((t, d), (s, d), (1, s)),
        out_specs=grid_one((t + s + 16, d))[0],
        scratch_shapes=[pltpu.VMEM((16, d), F32)],
        compiler_params=params(58),
        name="prepare",
    )(teach, stud, pairs)


def unit_kernel(place, v_hbm, unit_hbm, inv_ref, v, unit, sems_in, sems_out):
    chunks, _, width = v.shape

    def fetch(i):
        start = pl.multiple_of((place[0] * chunks + i) * width, width)
        return (pltpu.make_async_copy(v_hbm.at[:, pl.ds(start, width)], v.at[i], sems_in.at[i]),)

    def store(i):
        return pltpu.make_async_copy(unit.at[i], unit_hbm.at[i], sems_out.at[i])

    begin(chunks, fetch)

    def work(i):
        x = v[i].astype(F32)
        inv = lax.rsqrt(jnp.sum(x * x, axis=0, keepdims=True) + eps)
        unit[i] = (x * inv).astype(BF16)
        inv_ref[i] = inv
        store(i).start()

    stream(chunks, fetch, work)
    for i in range(chunks):
        store(i).wait()


def unit_call(place, v, kl):
    d = v.shape[0]
    shape = (CHUNKS, d, kl // CHUNKS)
    return pl.pallas_call(
        unit_kernel,
        out_shape=(
            jax.ShapeDtypeStruct(shape, BF16),
            jax.ShapeDtypeStruct((CHUNKS, 1, kl // CHUNKS), F32),
        ),
        in_specs=[SMEM] + anywhere(1),
        out_specs=tuple(anywhere(1) + vmem(1)),
        scratch_shapes=[pltpu.VMEM(shape, BF16), pltpu.VMEM(shape, BF16), DMA((CHUNKS,)), DMA((CHUNKS,))],
        cost_estimate=pl.CostEstimate(flops=4 * d * kl, bytes_accessed=4 * d * kl, transcendentals=kl),
        compiler_params=params(LIMIT),
        name="unit",
    )(place, v)


def energy_kernel(total_k, teach_ref, unit_hbm, energy_hbm, sum_ref, unit, energy, acc, sems_in, sems_out):
    chunks = unit.shape[0]

    def fetch(i):
        return (pltpu.make_async_copy(unit_hbm.at[i], unit.at[i], sems_in.at[i]),)

    def store(i):
        return pltpu.make_async_copy(energy.at[i], energy_hbm.at[i], sems_out.at[i])

    begin(chunks, fetch)
    acc[...] = jnp.zeros_like(acc)

    def work(i):
        dots = jnp.dot(teach_ref[...], unit[i], preferred_element_type=F32)
        e = jnp.exp2(dots * (LOG2E / teacher_temp))
        energy[i] = e.astype(BF16)
        store(i).start()
        col = 1.0 / (jnp.sum(e, axis=0, keepdims=True) * total_k)
        acc[...] += lane_sums(e * col)

    stream(chunks, fetch, work)
    sum_ref[...] = to_row(acc[...])
    for i in range(chunks):
        store(i).wait()


def energy_call(teach, unit, total_k):
    t, d = teach.shape
    chunks, _, width = unit.shape
    shape = (chunks, t, width)
    return pl.pallas_call(
        functools.partial(energy_kernel, float(total_k)),
        out_shape=(jax.ShapeDtypeStruct(shape, BF16), jax.ShapeDtypeStruct((1, t), F32)),
        in_specs=vmem(1) + anywhere(1),
        out_specs=tuple(anywhere(1) + vmem(1)),
        scratch_shapes=[
            pltpu.VMEM(unit.shape, BF16), pltpu.VMEM(shape, BF16), pltpu.VMEM((t, 128), F32),
            DMA((chunks,)), DMA((chunks,)),
        ],
        cost_estimate=pl.CostEstimate(
            flops=2 * t * d * chunks * width, bytes_accessed=4 * t * chunks * width, transcendentals=0
        ),
        compiler_params=params(LIMIT),
        name="energy",
    )(teach, unit)


def iterate_kernel(total_k, last, sum_in, energy_hbm, *refs):
    if last:
        unit_hbm, near_ref, far_ref, sum_ref, mean_ref, scaled_hbm = refs[:6]
        acc, row, energy, sems_in, scaled, unit, sems_out = refs[6:]
        mean_ref[...] = jnp.zeros_like(mean_ref)
    else:
        sum_ref, acc, row, energy, sems_in = refs
    chunks, t, width = energy.shape

    def fetch(i):
        copy = pltpu.make_async_copy(energy_hbm.at[i], energy.at[i], sems_in.at[i, 0])
        if not last:
            return (copy,)
        return (copy, pltpu.make_async_copy(unit_hbm.at[i], unit.at[i], sems_in.at[i, 1]))

    def store(i):
        return pltpu.make_async_copy(scaled.at[i], scaled_hbm.at[i], sems_out.at[i])

    begin(chunks, fetch)
    row[...] = to_column(1.0 / (sum_in[...] * float(t)))
    acc[...] = jnp.zeros_like(acc)

    def work(i):
        scale = row[...]
        col = []
        for at in range(0, width, 128):
            mass = jnp.sum(energy[i, :, at : at + 128].astype(F32) * scale, axis=0, keepdims=True)
            col.append(1.0 / (mass * total_k))
        part = None
        for n, at in enumerate(range(0, width, 128)):
            x = energy[i, :, at : at + 128].astype(F32) * col[n]
            if last:
                scaled[i, :, at : at + 128] = x.astype(BF16)
            part = x if part is None else part + x
        acc[...] += part
        if last:
            store(i).start()
            mean_ref[...] += lax.dot_general(unit[i], scaled[i], NT, preferred_element_type=F32)

    stream(chunks, fetch, work)
    sum_ref[:, :t] = to_row(acc[...])
    if last:
        n = near_ref.shape[1]
        sum_ref[:, t : t + n] = near_ref[...]
        sum_ref[:, t + n :] = far_ref[...]
        for i in range(chunks):
            store(i).wait()


def iterate_call(sums, energy, total_k, more=()):
    chunks, t, width = energy.shape
    last = bool(more)
    out_shape = [jax.ShapeDtypeStruct((1, t), F32)]
    in_specs, out_specs = vmem(1) + anywhere(1), vmem(1)
    scratch = [
        pltpu.VMEM((t, 128), F32), pltpu.VMEM((t, 128), F32), pltpu.VMEM(energy.shape, BF16), DMA((chunks, 2))
    ]
    if last:
        unit, near, far = more
        d = unit.shape[1]
        out_shape = [
            jax.ShapeDtypeStruct((1, t + near.shape[1] + far.shape[1]), F32),
            jax.ShapeDtypeStruct((d, t), F32),
            jax.ShapeDtypeStruct(energy.shape, BF16),
        ]
        in_specs, out_specs = in_specs + anywhere(1) + vmem(2), vmem(2) + anywhere(1)
        scratch += [pltpu.VMEM(energy.shape, BF16), pltpu.VMEM(unit.shape, BF16), DMA((chunks,))]
    return pl.pallas_call(
        functools.partial(iterate_kernel, float(total_k), last),
        out_shape=out_shape,
        in_specs=in_specs,
        out_specs=out_specs,
        scratch_shapes=scratch,
        cost_estimate=pl.CostEstimate(
            flops=4 * t * chunks * width, bytes_accessed=4 * t * chunks * width, transcendentals=0
        ),
        compiler_params=params(LIMIT),
        name="iterate_last" if last else "iterate",
    )(sums, energy, *more)


def student_kernel(block, near, rest_ref, pairs_ref, unit_hbm, expo_hbm, denom_ref, stud_t_ref, weight_ref, *refs):
    if near:
        pull_ref, pull, refs = refs[0], refs[-1], refs[1:-1]
        pull[...] = jnp.zeros_like(pull)
    unit, expo, acc, stud, sems_in, sems_out = refs
    chunks, s, width = expo.shape
    s_dev = s // rest_ref.shape[0]
    t = weight_ref.shape[1]

    def fetch(i):
        return (pltpu.make_async_copy(unit_hbm.at[i], unit.at[i], sems_in.at[i]),)

    def store(i):
        return pltpu.make_async_copy(expo.at[i], expo_hbm.at[i], sems_out.at[i])

    begin(chunks, fetch)
    acc[...] = jnp.zeros_like(acc)
    for i in range(rest_ref.shape[0]):
        stud[i * s_dev : (i + 1) * s_dev, :] = rest_ref[i, :s_dev, :]
    rows_t = stud[...].astype(F32).T.astype(BF16)
    stud_t_ref[...] = rows_t
    which = lax.broadcasted_iota(jnp.int32, (t, s), 0)
    onehot = (which == pairs_ref[...]).astype(F32).astype(BF16)
    weight_ref[...] = lax.dot_general(rows_t, onehot, NT, preferred_element_type=F32)

    def work(i):
        for at in range(0, s, block):
            logits = jnp.dot(stud[at : at + block, :], unit[i], preferred_element_type=F32)
            x = jnp.exp2(logits * (LOG2E / student_temp))
            expo[i, at : at + block, :] = x.astype(BF16)
            acc[at : at + block, :] += lane_sums(x)
        store(i).start()
        if near:
            pull[...] += lax.dot_general(expo[i], unit[i], NT, preferred_element_type=F32)

    stream(chunks, fetch, work)
    denom_ref[...] = to_row(acc[...])
    if near:
        pull_ref[...] = pull[...].T
    for i in range(chunks):
        store(i).wait()


def student_call(rest, pairs, unit, t, near):
    chunks, d, width = unit.shape
    s = rest.shape[0] * (rest.shape[1] - 16)
    shape = (chunks, s, width)
    out_shape = [
        jax.ShapeDtypeStruct(shape, BF16),
        jax.ShapeDtypeStruct((1, s), F32),
        jax.ShapeDtypeStruct((d, s), BF16),
        jax.ShapeDtypeStruct((d, t), F32),
    ]
    scratch = [
        pltpu.VMEM(unit.shape, BF16), pltpu.VMEM(shape, BF16), pltpu.VMEM((s, 128), F32),
        pltpu.VMEM((s, d), BF16), DMA((chunks,)), DMA((chunks,)),
    ]
    if near:
        out_shape += [jax.ShapeDtypeStruct((d, s), F32)]
        scratch += [pltpu.VMEM((s, d), F32)]
    return pl.pallas_call(
        functools.partial(student_kernel, 2 * (rest.shape[1] - 16), near),
        out_shape=out_shape,
        in_specs=vmem(2) + anywhere(1),
        out_specs=anywhere(1) + vmem(len(out_shape) - 1),
        scratch_shapes=scratch,
        cost_estimate=pl.CostEstimate(
            flops=4 * s * d * chunks * width, bytes_accessed=2 * s * chunks * width, transcendentals=0
        ),
        compiler_params=params(LIMIT),
        name="student_near" if near else "student_far",
    )(rest, pairs, unit)


def back_terms(factor, place, both_ref, pairs_ref, stud_t_ref, pull_ref, mean_ref, keep_ref, send_ref, tail_ref, back):
    d, n = pull_ref.shape
    t = mean_ref.shape[1]
    sums = both_ref[:, :t]
    denom = both_ref[:, t : t + n]
    row = 1.0 / (sums * float(t))
    pairs = pairs_ref[:, :n]
    mass = pick(to_column(row * sums * float(t)), pairs)
    which = lax.broadcasted_iota(jnp.int32, (t, n), 0)
    onehot = (which == pairs).astype(F32)
    target = jnp.dot(
        mean_ref[...] * (row * t), onehot, preferred_element_type=F32, precision=lax.Precision.HIGHEST
    )
    stud_t = stud_t_ref[...].astype(F32)
    terms = (pull_ref[...] * (mass / denom) - target) * factor
    back[...] = terms
    along = jnp.sum(stud_t * terms, axis=0, keepdims=True)
    cross = jnp.sum(stud_t * target, axis=0, keepdims=True) * (1.0 / student_temp)
    at = lax.broadcasted_iota(jnp.int32, (8, n), 0)
    tail = jnp.where(at == 0, along, jnp.where(at == 1, cross, 0.0))
    half = d // 2
    keep_ref[...] = back[pl.ds(pl.multiple_of(place[3] * half, half), half), :]
    send_ref[:half, :] = back[pl.ds(pl.multiple_of((1 - place[3]) * half, half), half), :]
    send_ref[half:, :] = tail
    tail_ref[...] = tail


def head_kernel(factor, first, place, both_ref, pairs_ref, near_ref, far_ref, weight_ref, more_weight_ref,
                inv_ref, near_hbm, far_hbm, scaled_hbm, v_hbm, *refs):
    if first == 0:
        pull_ref, mean_ref, own_hbm = refs[:3]
        sends, terms, refs = refs[3 : GROUP + 2], refs[GROUP + 2 : GROUP + 5], refs[GROUP + 5 :]
        back, refs = refs[-1], refs[:-1]
    else:
        own_hbm, sends, refs = refs[1], refs[2 : GROUP + 1], refs[GROUP + 1 :]
    lhs, lhs_teach, grad, expo, scaled, v, own, sems_in, sems_out = refs
    chunks, t, width = scaled.shape
    all_chunks = inv_ref.shape[0]
    n_near, n_far = near_ref.shape[1], far_ref.shape[1]
    rows = own.shape[1]

    def start_of(i):
        return pl.multiple_of((place[0] * all_chunks + first + i) * width, width)

    def fetches(i):
        return (
            pltpu.make_async_copy(near_hbm.at[first + i], expo.at[i, pl.ds(0, n_near), :], sems_in.at[i, 0]),
            pltpu.make_async_copy(far_hbm.at[first + i], expo.at[i, pl.ds(n_near, n_far), :], sems_in.at[i, 3]),
            pltpu.make_async_copy(scaled_hbm.at[first + i], scaled.at[i], sems_in.at[i, 1]),
            pltpu.make_async_copy(v_hbm.at[:, pl.ds(start_of(i), width)], v.at[i], sems_in.at[i, 2]),
        )

    def store(i):
        return pltpu.make_async_copy(own.at[i], own_hbm.at[:, pl.ds(start_of(i), width)], sems_out.at[i])

    begin(chunks, fetches)
    sums, denom = both_ref[:, :t], both_ref[:, t:]
    row = 1.0 / (sums * float(t))
    mass = pick(to_column(row * sums * float(t)), pairs_ref[...])
    scale = mass / denom * factor
    lhs[:, :n_near] = (near_ref[...].astype(F32) * scale[:, :n_near]).astype(BF16)
    lhs[:, n_near:] = (far_ref[...].astype(F32) * scale[:, n_near:]).astype(BF16)
    lhs_teach[...] = ((weight_ref[...] + more_weight_ref[...]) * (row * (-factor * t))).astype(BF16)
    if first == 0:
        back_terms(factor, place, both_ref, pairs_ref, near_ref, pull_ref, mean_ref, *terms, back)
    base = place[1] * (rows * GROUP)

    def part(n):
        start = pl.multiple_of(base + (place[0] ^ n) * rows, rows)
        return grad[pl.ds(start, rows), :]

    def work(i):
        head = jnp.dot(lhs[...], expo[i], preferred_element_type=F32)
        head = head + jnp.dot(lhs_teach[...], scaled[i], preferred_element_type=F32)
        inv = inv_ref[first + i]
        unit = v[i].astype(F32) * inv
        proj = jnp.sum(unit * head, axis=0, keepdims=True)
        grad[...] = (head - unit * proj) * inv
        own[i] = part(0)
        store(i).start()
        at = pl.ds(pl.multiple_of(i * width, width), width)
        for n, ref in enumerate(sends):
            ref[:, at] = part(n + 1).astype(BF16)

    stream(chunks, fetches, work)
    for i in range(chunks):
        store(i).wait()


def head_call(first, chunks, place, both, pairs, students, inv, scaled, v, factor, rows, more):
    near, far, near_t, far_t, weight, more_weight = students
    d, s = near_t.shape[0], pairs.shape[1]
    _, t, width = scaled.shape
    kl = chunks * width
    out_shape = [jax.ShapeDtypeStruct((rows, v.shape[1]), F32)] + [jax.ShapeDtypeStruct((rows, kl), BF16)] * (GROUP - 1)
    out_specs = anywhere(1) + vmem(GROUP - 1)
    scratch = [
        pltpu.VMEM((d, s), BF16), pltpu.VMEM((d, t), BF16), pltpu.VMEM((d, width), F32),
        pltpu.VMEM((chunks, s, width), BF16), pltpu.VMEM((chunks, t, width), BF16),
        pltpu.VMEM((chunks, d, width), BF16), pltpu.VMEM((chunks, rows, width), F32),
        DMA((chunks, 4)), DMA((chunks,)),
    ]
    if first == 0:
        n = more[0].shape[1]
        out_shape += [
            jax.ShapeDtypeStruct((d // 2, n), F32),
            jax.ShapeDtypeStruct((d // 2 + 8, n), F32),
            jax.ShapeDtypeStruct((8, n), F32),
        ]
        out_specs += vmem(3)
        scratch += [pltpu.VMEM((d, n), F32)]
    return pl.pallas_call(
        functools.partial(head_kernel, factor, first),
        out_shape=out_shape,
        in_specs=[SMEM] + vmem(7) + anywhere(4) + (vmem(2) if first == 0 else anywhere(1)),
        out_specs=out_specs,
        scratch_shapes=scratch,
        input_output_aliases={} if first == 0 else {12: 0},
        cost_estimate=pl.CostEstimate(
            flops=4 * (s + t) * d * kl, bytes_accessed=2 * (s + t + d) * kl, transcendentals=0
        ),
        compiler_params=params(LIMIT),
        name="head",
    )(place, both, pairs, near_t, far_t, weight, more_weight, inv, near, far, scaled, v, *more)


def finish_kernel(t, place, both_ref, denom_ref, pairs_ref, stud_ref, *refs):
    terms, (grad_ref, loss_ref, unit) = refs[:GROUP], refs[GROUP:]
    total = (terms[0][...] + terms[1][...]) + (terms[2][...] + terms[3][...])
    share = grad_ref.shape[0]
    x = stud_ref[...].astype(F32).T
    norm = jnp.sqrt(jnp.sum(x * x, axis=0, keepdims=True) + eps)
    unit[...] = x / norm
    part = unit[pl.ds(pl.multiple_of(place[2] * share, share), share), :]
    along, cross = total[share : share + 1, :], total[share + 1 : share + 2, :]
    grad_ref[...] = (total[:share, :] - part * along) / norm
    sums = both_ref[:, :t]
    mass = pick(to_column(1.0 / (sums * float(t)) * sums * float(t)), pairs_ref[...])
    loss_ref[...] = jnp.log(denom_ref[...]) * mass - cross


def finish_call(t, place, both, denom, pairs, stud, terms, share):
    s, d = stud.shape
    return pl.pallas_call(
        functools.partial(finish_kernel, t),
        out_shape=(jax.ShapeDtypeStruct((share, s), F32), jax.ShapeDtypeStruct((1, s), F32)),
        in_specs=[SMEM] + vmem(4 + GROUP),
        out_specs=tuple(vmem(2)),
        scratch_shapes=[pltpu.VMEM((d, s), F32)],
        compiler_params=params(8),
        name="finish",
    )(place, both, denom, pairs, stud, *terms)


def body(teacher_features, student_features, v, pairing):
    n_rows, n_proto = lax.axis_size("rows"), lax.axis_size("proto")
    r, p = lax.axis_index("rows"), lax.axis_index("proto")
    d, local_k = v.shape
    total_k = local_k * n_proto
    kl = local_k // GROUP
    t_dev, s_dev = teacher_features.shape[0], student_features.shape[0]
    t, s = t_dev * n_rows, s_dev * n_rows
    at, group = r % GROUP, r // GROUP
    top = (p * 2) // n_proto
    place = jnp.stack([at, group, p, top]).astype(jnp.int32)
    factor = total_k / 64.0 / student_temp

    def swap_rows(x, n):
        return lax.ppermute(x, "rows", [(j, j ^ n) for j in range(n_rows)])

    def swap_proto(x, n):
        return lax.ppermute(x, "proto", [(j, j ^ n) for j in range(n_proto)])

    def total(x):
        for swap, size in ((swap_proto, n_proto), (swap_rows, GROUP)):
            n = 1
            while n < size:
                x = (x + swap(x, n)) + (swap(x, 2 * n) + swap(x, 3 * n))
                n *= 4
        return x

    def join(x, n, other=None):
        other = swap_rows(x, n) if other is None else other
        low = (r // n) % 2 == 0
        return jnp.concatenate([jnp.where(low, x, other), jnp.where(low, other, x)], axis=0)

    own_pairs = pairing.reshape(1, s_dev)
    unit, inv = unit_call(place, v, kl)
    packed = prepare_call(teacher_features, student_features, own_pairs)[None]
    packed = join(packed, 1)
    other, unit, inv = lax.optimization_barrier((swap_rows(packed, 2), unit, inv))
    packed = join(packed, 2, other)
    teach_all, near = packed[:, :t_dev], packed[:, t_dev:]
    n = GROUP
    while n < n_rows:
        teach_all = join(teach_all, n)
        n *= 2
    teach_all = teach_all.reshape(t, d)

    def pairs_of(rest):
        digits = rest[:, s_dev : s_dev + 2, :s_dev].astype(F32)
        return (digits[:, 0] * 64.0 + digits[:, 1]).astype(jnp.int32).reshape(1, -1)

    energy, sums = energy_call(teach_all, unit, total_k)
    far = swap_rows(near, GROUP)
    n = 2 * GROUP
    while n < n_rows:
        far = jnp.concatenate([far, swap_rows(jnp.concatenate([near, far], axis=0), n)], axis=0)
        n *= 2
    near_pairs = pairs_of(near)
    expo_near, denom_near, near_t, weight, pull = student_call(near, near_pairs, unit, t, True)
    sums = total(sums)
    far, denom_near, sums = lax.optimization_barrier((far, denom_near, sums))
    far_pairs = pairs_of(far)
    expo_far, denom_far, far_t, more_weight = student_call(far, far_pairs, unit, t, False)
    pairs = jnp.concatenate([near_pairs, far_pairs], axis=1)
    (sums,) = iterate_call(sums, energy, total_k)
    both, mean, scaled = iterate_call(total(sums), energy, total_k, (unit, denom_near, denom_far))
    both = total(both)
    students = (expo_near, expo_far, near_t, far_t, weight, more_weight)

    rows = d // n_rows
    chunks = CHUNKS // PARTS
    more = (pull, mean)
    pieces = []
    for first in range(0, CHUNKS, chunks):
        out = head_call(
            first, chunks, place, both, pairs, students, inv, scaled, v, factor, rows, more
        )
        if first == 0:
            body_rows, send, tail = out[GROUP:]
        more = (out[0],)
        arrived = []
        for n in range(1, GROUP):
            share = out[n]
            if pieces:
                share, pieces[-1][n - 1] = lax.optimization_barrier((share, pieces[-1][n - 1]))
            arrived.append(swap_rows(share, n))
        pieces.append(arrived)
    proto_grad = out[0]
    for part, arrived in enumerate(pieces):
        for n, got in enumerate(arrived, 1):
            start = (at ^ n) * kl + part * (kl // PARTS)
            proto_grad = lax.dynamic_update_slice(proto_grad, got.astype(F32), (0, start))

    n = n_proto // 2
    while n >= 1:
        if n < n_proto // 2:
            height = body_rows.shape[0] // 2
            bit = (p // n) % 2
            send = lax.dynamic_slice_in_dim(body_rows, (1 - bit) * height, height, 0)
            body_rows = lax.dynamic_slice_in_dim(body_rows, bit * height, height, 0)
            send = jnp.concatenate([send, tail], axis=0)
        got = swap_proto(send, n)
        height = body_rows.shape[0]
        body_rows, tail = body_rows + got[:height], tail + got[height:]
        n //= 2
    terms = jnp.concatenate([body_rows, tail], axis=0)

    def block(n):
        return lax.dynamic_slice_in_dim(terms, (at ^ n) * s_dev, s_dev, 1)

    parts = [block(0)] + [swap_rows(block(n), n) for n in range(1, GROUP)]
    own = lax.dynamic_slice_in_dim(both, t + at * s_dev, s_dev, 1)
    student_grad, loss = finish_call(t, place, both, own, own_pairs, student_features, parts, d // n_proto)
    return (proto_grad, student_grad.T, loss.reshape(s_dev))


def solution(mesh):
    return jax.shard_map(
        body,
        mesh=mesh,
        in_specs=(P("rows", None), P("rows", None), P(None, "proto"), P("rows")),
        out_specs=(P("rows", "proto"), P("rows", "proto"), P("rows")),
        check_vma=False,
    )
```

```python
import functools

import jax
import jax.numpy as jnp
from jax import lax
from jax.experimental import pallas as pl
from jax.experimental.pallas import tpu as pltpu
from jax.sharding import PartitionSpec as P

teacher_temp = 0.07
student_temp = 0.1
eps = 1e-06
LOG2E = 1.4426950408889634
GROUP = 4
CHUNKS = 8
LIMIT = 50
PARTS = 2
F32 = jnp.float32
BF16 = jnp.bfloat16
NT = (((1,), (1,)), ((), ()))


def params(mib):
    return pltpu.CompilerParams(vmem_limit_bytes=mib * 1024 * 1024)


def vmem(count):
    return [pl.BlockSpec(memory_space=pltpu.VMEM)] * count


def anywhere(count):
    return [pl.BlockSpec(memory_space=pl.ANY)] * count


def grid_one(*shapes):
    return [pl.BlockSpec(shape, lambda i, n=len(shape): (0,) * n) for shape in shapes]


SMEM = pl.BlockSpec(memory_space=pltpu.SMEM)
DMA = pltpu.SemaphoreType.DMA
AHEAD = 3


def begin(chunks, fetch):
    for i in range(min(AHEAD, chunks)):
        for copy in fetch(i):
            copy.start()


def stream(chunks, fetch, work):
    @pl.loop(0, chunks)
    def _(i):
        @pl.when(i + AHEAD < chunks)
        def _():
            for copy in fetch(i + AHEAD):
                copy.start()

        for copy in fetch(i):
            copy.wait()
        work(i)


def to_column(row):
    return jnp.broadcast_to(row, (128, row.shape[1])).T


def lane_sums(x):
    total = x[:, :128]
    for at in range(128, x.shape[1], 128):
        total = total + x[:, at : at + 128]
    return total


def to_row(acc):
    return jnp.sum(acc.T, axis=0, keepdims=True)


def pick(column, pairs):
    t, n = column.shape[0], pairs.shape[1]
    out = []
    for at in range(0, n, 128):
        width = min(128, n - at)
        which = lax.broadcasted_iota(jnp.int32, (t, width), 0)
        hit = which == pairs[:, at : at + width]
        out.append(jnp.sum(jnp.where(hit, column[:, :width], 0.0), axis=0, keepdims=True))
    return jnp.concatenate(out, axis=1)


def prepare_kernel(teach_ref, stud_ref, pairs_ref, out_ref, digits):
    t, s = teach_ref.shape[0], stud_ref.shape[0]
    for ref, at, n in ((teach_ref, 0, t), (stud_ref, t, s)):
        x = ref[...].astype(F32)
        norm = jnp.sqrt(jnp.sum(x * x, axis=1, keepdims=True) + eps)
        out_ref[at : at + n, :] = (x / norm).astype(BF16)
    pairs = pairs_ref[...]
    high = lax.shift_right_logical(pairs, 6)
    row = lax.broadcasted_iota(jnp.int32, (16, s), 0)
    digits[...] = jnp.zeros_like(digits)
    digits[:, :s] = jnp.where(row == 0, high, jnp.where(row == 1, pairs - high * 64, 0)).astype(F32)
    out_ref[t + s :, :] = digits[...].astype(BF16)


def prepare_call(teach, stud, pairs):
    t, s, d = teach.shape[0], stud.shape[0], stud.shape[1]
    return pl.pallas_call(
        prepare_kernel,
        out_shape=jax.ShapeDtypeStruct((t + s + 16, d), BF16),
        grid=(1,),
        in_specs=grid_one((t, d), (s, d), (1, s)),
        out_specs=grid_one((t + s + 16, d))[0],
        scratch_shapes=[pltpu.VMEM((16, d), F32)],
        compiler_params=params(58),
        name="prepare",
    )(teach, stud, pairs)


def unit_kernel(place, v_hbm, unit_hbm, inv_ref, v, unit, sems_in, sems_out):
    chunks, _, width = v.shape

    def fetch(i):
        start = pl.multiple_of((place[0] * chunks + i) * width, width)
        return (pltpu.make_async_copy(v_hbm.at[:, pl.ds(start, width)], v.at[i], sems_in.at[i]),)

    def store(i):
        return pltpu.make_async_copy(unit.at[i], unit_hbm.at[i], sems_out.at[i])

    begin(chunks, fetch)

    def work(i):
        x = v[i].astype(F32)
        inv = lax.rsqrt(jnp.sum(x * x, axis=0, keepdims=True) + eps)
        unit[i] = (x * inv).astype(BF16)
        inv_ref[i] = inv
        store(i).start()

    stream(chunks, fetch, work)
    for i in range(chunks):
        store(i).wait()


def unit_call(place, v, kl):
    d = v.shape[0]
    shape = (CHUNKS, d, kl // CHUNKS)
    return pl.pallas_call(
        unit_kernel,
        out_shape=(
            jax.ShapeDtypeStruct(shape, BF16),
            jax.ShapeDtypeStruct((CHUNKS, 1, kl // CHUNKS), F32),
        ),
        in_specs=[SMEM] + anywhere(1),
        out_specs=tuple(anywhere(1) + vmem(1)),
        scratch_shapes=[pltpu.VMEM(shape, BF16), pltpu.VMEM(shape, BF16), DMA((CHUNKS,)), DMA((CHUNKS,))],
        cost_estimate=pl.CostEstimate(flops=4 * d * kl, bytes_accessed=4 * d * kl, transcendentals=kl),
        compiler_params=params(LIMIT),
        name="unit",
    )(place, v)


def energy_kernel(total_k, teach_ref, unit_hbm, energy_hbm, sum_ref, unit, energy, acc, sems_in, sems_out):
    chunks = unit.shape[0]

    def fetch(i):
        return (pltpu.make_async_copy(unit_hbm.at[i], unit.at[i], sems_in.at[i]),)

    def store(i):
        return pltpu.make_async_copy(energy.at[i], energy_hbm.at[i], sems_out.at[i])

    begin(chunks, fetch)
    acc[...] = jnp.zeros_like(acc)

    def work(i):
        dots = jnp.dot(teach_ref[...], unit[i], preferred_element_type=F32)
        e = jnp.exp2(dots * (LOG2E / teacher_temp))
        energy[i] = e.astype(BF16)
        store(i).start()
        col = 1.0 / (jnp.sum(e, axis=0, keepdims=True) * total_k)
        acc[...] += lane_sums(e * col)

    stream(chunks, fetch, work)
    sum_ref[...] = to_row(acc[...])
    for i in range(chunks):
        store(i).wait()


def energy_call(teach, unit, total_k):
    t, d = teach.shape
    chunks, _, width = unit.shape
    shape = (chunks, t, width)
    return pl.pallas_call(
        functools.partial(energy_kernel, float(total_k)),
        out_shape=(jax.ShapeDtypeStruct(shape, BF16), jax.ShapeDtypeStruct((1, t), F32)),
        in_specs=vmem(1) + anywhere(1),
        out_specs=tuple(anywhere(1) + vmem(1)),
        scratch_shapes=[
            pltpu.VMEM(unit.shape, BF16), pltpu.VMEM(shape, BF16), pltpu.VMEM((t, 128), F32),
            DMA((chunks,)), DMA((chunks,)),
        ],
        cost_estimate=pl.CostEstimate(
            flops=2 * t * d * chunks * width, bytes_accessed=4 * t * chunks * width, transcendentals=0
        ),
        compiler_params=params(LIMIT),
        name="energy",
    )(teach, unit)


def iterate_kernel(total_k, last, sum_in, energy_hbm, *refs):
    if last:
        unit_hbm, near_ref, far_ref, sum_ref, mean_ref, scaled_hbm = refs[:6]
        acc, row, energy, sems_in, scaled, unit, sems_out = refs[6:]
        mean_ref[...] = jnp.zeros_like(mean_ref)
    else:
        sum_ref, acc, row, energy, sems_in = refs
    chunks, t, width = energy.shape

    def fetch(i):
        copy = pltpu.make_async_copy(energy_hbm.at[i], energy.at[i], sems_in.at[i, 0])
        if not last:
            return (copy,)
        return (copy, pltpu.make_async_copy(unit_hbm.at[i], unit.at[i], sems_in.at[i, 1]))

    def store(i):
        return pltpu.make_async_copy(scaled.at[i], scaled_hbm.at[i], sems_out.at[i])

    begin(chunks, fetch)
    row[...] = to_column(1.0 / (sum_in[...] * float(t)))
    acc[...] = jnp.zeros_like(acc)

    def work(i):
        scale = row[...]
        col = []
        for at in range(0, width, 128):
            mass = jnp.sum(energy[i, :, at : at + 128].astype(F32) * scale, axis=0, keepdims=True)
            col.append(1.0 / (mass * total_k))
        part = None
        for n, at in enumerate(range(0, width, 128)):
            x = energy[i, :, at : at + 128].astype(F32) * col[n]
            if last:
                scaled[i, :, at : at + 128] = x.astype(BF16)
            part = x if part is None else part + x
        acc[...] += part
        if last:
            store(i).start()
            mean_ref[...] += lax.dot_general(unit[i], scaled[i], NT, preferred_element_type=F32)

    stream(chunks, fetch, work)
    sum_ref[:, :t] = to_row(acc[...])
    if last:
        n = near_ref.shape[1]
        sum_ref[:, t : t + n] = near_ref[...]
        sum_ref[:, t + n :] = far_ref[...]
        for i in range(chunks):
            store(i).wait()


def iterate_call(sums, energy, total_k, more=()):
    chunks, t, width = energy.shape
    last = bool(more)
    out_shape = [jax.ShapeDtypeStruct((1, t), F32)]
    in_specs, out_specs = vmem(1) + anywhere(1), vmem(1)
    scratch = [
        pltpu.VMEM((t, 128), F32), pltpu.VMEM((t, 128), F32), pltpu.VMEM(energy.shape, BF16), DMA((chunks, 2))
    ]
    if last:
        unit, near, far = more
        d = unit.shape[1]
        out_shape = [
            jax.ShapeDtypeStruct((1, t + near.shape[1] + far.shape[1]), F32),
            jax.ShapeDtypeStruct((d, t), F32),
            jax.ShapeDtypeStruct(energy.shape, BF16),
        ]
        in_specs, out_specs = in_specs + anywhere(1) + vmem(2), vmem(2) + anywhere(1)
        scratch += [pltpu.VMEM(energy.shape, BF16), pltpu.VMEM(unit.shape, BF16), DMA((chunks,))]
    return pl.pallas_call(
        functools.partial(iterate_kernel, float(total_k), last),
        out_shape=out_shape,
        in_specs=in_specs,
        out_specs=out_specs,
        scratch_shapes=scratch,
        cost_estimate=pl.CostEstimate(
            flops=4 * t * chunks * width, bytes_accessed=4 * t * chunks * width, transcendentals=0
        ),
        compiler_params=params(LIMIT),
        name="iterate_last" if last else "iterate",
    )(sums, energy, *more)


def student_kernel(block, near, rest_ref, pairs_ref, unit_hbm, expo_hbm, denom_ref, stud_t_ref, weight_ref, *refs):
    if near:
        pull_ref, pull, refs = refs[0], refs[-1], refs[1:-1]
        pull[...] = jnp.zeros_like(pull)
    unit, expo, acc, stud, sems_in, sems_out = refs
    chunks, s, width = expo.shape
    s_dev = s // rest_ref.shape[0]
    t = weight_ref.shape[1]

    def fetch(i):
        return (pltpu.make_async_copy(unit_hbm.at[i], unit.at[i], sems_in.at[i]),)

    def store(i):
        return pltpu.make_async_copy(expo.at[i], expo_hbm.at[i], sems_out.at[i])

    begin(chunks, fetch)
    acc[...] = jnp.zeros_like(acc)
    for i in range(rest_ref.shape[0]):
        stud[i * s_dev : (i + 1) * s_dev, :] = rest_ref[i, :s_dev, :]
    rows_t = stud[...].astype(F32).T.astype(BF16)
    stud_t_ref[...] = rows_t
    which = lax.broadcasted_iota(jnp.int32, (t, s), 0)
    onehot = (which == pairs_ref[...]).astype(F32).astype(BF16)
    weight_ref[...] = lax.dot_general(rows_t, onehot, NT, preferred_element_type=F32)

    def work(i):
        for at in range(0, s, block):
            logits = jnp.dot(stud[at : at + block, :], unit[i], preferred_element_type=F32)
            x = jnp.exp2(logits * (LOG2E / student_temp))
            expo[i, at : at + block, :] = x.astype(BF16)
            acc[at : at + block, :] += lane_sums(x)
        store(i).start()
        if near:
            pull[...] += lax.dot_general(expo[i], unit[i], NT, preferred_element_type=F32)

    stream(chunks, fetch, work)
    denom_ref[...] = to_row(acc[...])
    if near:
        pull_ref[...] = pull[...].T
    for i in range(chunks):
        store(i).wait()


def student_call(rest, pairs, unit, t, near):
    chunks, d, width = unit.shape
    s = rest.shape[0] * (rest.shape[1] - 16)
    shape = (chunks, s, width)
    out_shape = [
        jax.ShapeDtypeStruct(shape, BF16),
        jax.ShapeDtypeStruct((1, s), F32),
        jax.ShapeDtypeStruct((d, s), BF16),
        jax.ShapeDtypeStruct((d, t), F32),
    ]
    scratch = [
        pltpu.VMEM(unit.shape, BF16), pltpu.VMEM(shape, BF16), pltpu.VMEM((s, 128), F32),
        pltpu.VMEM((s, d), BF16), DMA((chunks,)), DMA((chunks,)),
    ]
    if near:
        out_shape += [jax.ShapeDtypeStruct((d, s), F32)]
        scratch += [pltpu.VMEM((s, d), F32)]
    return pl.pallas_call(
        functools.partial(student_kernel, 2 * (rest.shape[1] - 16), near),
        out_shape=out_shape,
        in_specs=vmem(2) + anywhere(1),
        out_specs=anywhere(1) + vmem(len(out_shape) - 1),
        scratch_shapes=scratch,
        cost_estimate=pl.CostEstimate(
            flops=4 * s * d * chunks * width, bytes_accessed=2 * s * chunks * width, transcendentals=0
        ),
        compiler_params=params(LIMIT),
        name="student_near" if near else "student_far",
    )(rest, pairs, unit)


def back_terms(factor, place, both_ref, pairs_ref, stud_t_ref, pull_ref, mean_ref, keep_ref, send_ref, tail_ref, back):
    d, n = pull_ref.shape
    t = mean_ref.shape[1]
    sums = both_ref[:, :t]
    denom = both_ref[:, t : t + n]
    row = 1.0 / (sums * float(t))
    pairs = pairs_ref[:, :n]
    mass = pick(to_column(row * sums * float(t)), pairs)
    which = lax.broadcasted_iota(jnp.int32, (t, n), 0)
    onehot = (which == pairs).astype(F32)
    target = jnp.dot(
        mean_ref[...] * (row * t), onehot, preferred_element_type=F32, precision=lax.Precision.HIGHEST
    )
    stud_t = stud_t_ref[...].astype(F32)
    terms = (pull_ref[...] * (mass / denom) - target) * factor
    back[...] = terms
    along = jnp.sum(stud_t * terms, axis=0, keepdims=True)
    cross = jnp.sum(stud_t * target, axis=0, keepdims=True) * (1.0 / student_temp)
    at = lax.broadcasted_iota(jnp.int32, (8, n), 0)
    tail = jnp.where(at == 0, along, jnp.where(at == 1, cross, 0.0))
    half = d // 2
    keep_ref[...] = back[pl.ds(pl.multiple_of(place[3] * half, half), half), :]
    send_ref[:half, :] = back[pl.ds(pl.multiple_of((1 - place[3]) * half, half), half), :]
    send_ref[half:, :] = tail
    tail_ref[...] = tail


def head_kernel(factor, first, place, both_ref, pairs_ref, near_ref, far_ref, weight_ref, more_weight_ref,
                inv_ref, near_hbm, far_hbm, scaled_hbm, v_hbm, *refs):
    if first == 0:
        pull_ref, mean_ref, own_hbm = refs[:3]
        sends, terms, refs = refs[3 : GROUP + 2], refs[GROUP + 2 : GROUP + 5], refs[GROUP + 5 :]
        back, refs = refs[-1], refs[:-1]
    else:
        own_hbm, sends, refs = refs[1], refs[2 : GROUP + 1], refs[GROUP + 1 :]
    lhs, lhs_teach, grad, expo, scaled, v, own, sems_in, sems_out = refs
    chunks, t, width = scaled.shape
    all_chunks = inv_ref.shape[0]
    n_near, n_far = near_ref.shape[1], far_ref.shape[1]
    rows = own.shape[1]

    def start_of(i):
        return pl.multiple_of((place[0] * all_chunks + first + i) * width, width)

    def fetches(i):
        return (
            pltpu.make_async_copy(near_hbm.at[first + i], expo.at[i, pl.ds(0, n_near), :], sems_in.at[i, 0]),
            pltpu.make_async_copy(far_hbm.at[first + i], expo.at[i, pl.ds(n_near, n_far), :], sems_in.at[i, 3]),
            pltpu.make_async_copy(scaled_hbm.at[first + i], scaled.at[i], sems_in.at[i, 1]),
            pltpu.make_async_copy(v_hbm.at[:, pl.ds(start_of(i), width)], v.at[i], sems_in.at[i, 2]),
        )

    def store(i):
        return pltpu.make_async_copy(own.at[i], own_hbm.at[:, pl.ds(start_of(i), width)], sems_out.at[i])

    begin(chunks, fetches)
    sums, denom = both_ref[:, :t], both_ref[:, t:]
    row = 1.0 / (sums * float(t))
    mass = pick(to_column(row * sums * float(t)), pairs_ref[...])
    scale = mass / denom * factor
    lhs[:, :n_near] = (near_ref[...].astype(F32) * scale[:, :n_near]).astype(BF16)
    lhs[:, n_near:] = (far_ref[...].astype(F32) * scale[:, n_near:]).astype(BF16)
    lhs_teach[...] = ((weight_ref[...] + more_weight_ref[...]) * (row * (-factor * t))).astype(BF16)
    if first == 0:
        back_terms(factor, place, both_ref, pairs_ref, near_ref, pull_ref, mean_ref, *terms, back)
    base = place[1] * (rows * GROUP)

    def part(n):
        start = pl.multiple_of(base + (place[0] ^ n) * rows, rows)
        return grad[pl.ds(start, rows), :]

    def work(i):
        head = jnp.dot(lhs[...], expo[i], preferred_element_type=F32)
        head = head + jnp.dot(lhs_teach[...], scaled[i], preferred_element_type=F32)
        inv = inv_ref[first + i]
        unit = v[i].astype(F32) * inv
        proj = jnp.sum(unit * head, axis=0, keepdims=True)
        grad[...] = (head - unit * proj) * inv
        own[i] = part(0)
        store(i).start()
        at = pl.ds(pl.multiple_of(i * width, width), width)
        for n, ref in enumerate(sends):
            ref[:, at] = part(n + 1).astype(BF16)

    stream(chunks, fetches, work)
    for i in range(chunks):
        store(i).wait()


def head_call(first, chunks, place, both, pairs, students, inv, scaled, v, factor, rows, more):
    near, far, near_t, far_t, weight, more_weight = students
    d, s = near_t.shape[0], pairs.shape[1]
    _, t, width = scaled.shape
    kl = chunks * width
    out_shape = [jax.ShapeDtypeStruct((rows, v.shape[1]), F32)] + [jax.ShapeDtypeStruct((rows, kl), BF16)] * (GROUP - 1)
    out_specs = anywhere(1) + vmem(GROUP - 1)
    scratch = [
        pltpu.VMEM((d, s), BF16), pltpu.VMEM((d, t), BF16), pltpu.VMEM((d, width), F32),
        pltpu.VMEM((chunks, s, width), BF16), pltpu.VMEM((chunks, t, width), BF16),
        pltpu.VMEM((chunks, d, width), BF16), pltpu.VMEM((chunks, rows, width), F32),
        DMA((chunks, 4)), DMA((chunks,)),
    ]
    if first == 0:
        n = more[0].shape[1]
        out_shape += [
            jax.ShapeDtypeStruct((d // 2, n), F32),
            jax.ShapeDtypeStruct((d // 2 + 8, n), F32),
            jax.ShapeDtypeStruct((8, n), F32),
        ]
        out_specs += vmem(3)
        scratch += [pltpu.VMEM((d, n), F32)]
    return pl.pallas_call(
        functools.partial(head_kernel, factor, first),
        out_shape=out_shape,
        in_specs=[SMEM] + vmem(7) + anywhere(4) + (vmem(2) if first == 0 else anywhere(1)),
        out_specs=out_specs,
        scratch_shapes=scratch,
        input_output_aliases={} if first == 0 else {12: 0},
        cost_estimate=pl.CostEstimate(
            flops=4 * (s + t) * d * kl, bytes_accessed=2 * (s + t + d) * kl, transcendentals=0
        ),
        compiler_params=params(LIMIT),
        name="head",
    )(place, both, pairs, near_t, far_t, weight, more_weight, inv, near, far, scaled, v, *more)


def finish_kernel(t, place, both_ref, denom_ref, pairs_ref, stud_ref, *refs):
    terms, (grad_ref, loss_ref, unit) = refs[:GROUP], refs[GROUP:]
    total = (terms[0][...] + terms[1][...]) + (terms[2][...] + terms[3][...])
    share = grad_ref.shape[0]
    x = stud_ref[...].astype(F32).T
    norm = jnp.sqrt(jnp.sum(x * x, axis=0, keepdims=True) + eps)
    unit[...] = x / norm
    part = unit[pl.ds(pl.multiple_of(place[2] * share, share), share), :]
    along, cross = total[share : share + 1, :], total[share + 1 : share + 2, :]
    grad_ref[...] = (total[:share, :] - part * along) / norm
    sums = both_ref[:, :t]
    mass = pick(to_column(1.0 / (sums * float(t)) * sums * float(t)), pairs_ref[...])
    loss_ref[...] = jnp.log(denom_ref[...]) * mass - cross


def finish_call(t, place, both, denom, pairs, stud, terms, share):
    s, d = stud.shape
    return pl.pallas_call(
        functools.partial(finish_kernel, t),
        out_shape=(jax.ShapeDtypeStruct((share, s), F32), jax.ShapeDtypeStruct((1, s), F32)),
        in_specs=[SMEM] + vmem(4 + GROUP),
        out_specs=tuple(vmem(2)),
        scratch_shapes=[pltpu.VMEM((d, s), F32)],
        compiler_params=params(8),
        name="finish",
    )(place, both, denom, pairs, stud, *terms)


def body(teacher_features, student_features, v, pairing):
    n_rows, n_proto = lax.axis_size("rows"), lax.axis_size("proto")
    r, p = lax.axis_index("rows"), lax.axis_index("proto")
    d, local_k = v.shape
    total_k = local_k * n_proto
    kl = local_k // GROUP
    t_dev, s_dev = teacher_features.shape[0], student_features.shape[0]
    t, s = t_dev * n_rows, s_dev * n_rows
    at, group = r % GROUP, r // GROUP
    top = (p * 2) // n_proto
    place = jnp.stack([at, group, p, top]).astype(jnp.int32)
    factor = total_k / 64.0 / student_temp

    def swap_rows(x, n):
        return lax.ppermute(x, "rows", [(j, j ^ n) for j in range(n_rows)])

    def swap_proto(x, n):
        return lax.ppermute(x, "proto", [(j, j ^ n) for j in range(n_proto)])

    def total(x):
        for swap, size in ((swap_proto, n_proto), (swap_rows, GROUP)):
            n = 1
            while n < size:
                x = (x + swap(x, n)) + (swap(x, 2 * n) + swap(x, 3 * n))
                n *= 4
        return x

    def join(x, n, other=None):
        other = swap_rows(x, n) if other is None else other
        low = (r // n) % 2 == 0
        return jnp.concatenate([jnp.where(low, x, other), jnp.where(low, other, x)], axis=0)

    own_pairs = pairing.reshape(1, s_dev)
    unit, inv = unit_call(place, v, kl)
    packed = prepare_call(teacher_features, student_features, own_pairs)
    blocks = [packed] + [swap_rows(packed, n) for n in range(1, GROUP)]
    blocks[-1], unit, inv = lax.optimization_barrier((blocks[-1], unit, inv))
    for n in (1, 2):
        low = (at // n) % 2 == 0
        blocks = [jnp.where(low, blocks[j], blocks[j ^ n]) for j in range(GROUP)]
    packed = jnp.stack(blocks)
    teach_all, near = packed[:, :t_dev], packed[:, t_dev:]

    def pairs_of(rest):
        digits = rest[:, s_dev : s_dev + 2, :s_dev].astype(F32)
        return (digits[:, 0] * 64.0 + digits[:, 1]).astype(jnp.int32).reshape(1, -1)

    near_pairs = pairs_of(near)
    expo_near, denom_near, near_t, weight, pull = student_call(near, near_pairs, unit, t, True)
    n = GROUP
    while n < n_rows:
        other = swap_rows(teach_all, n)
        teach_all = join(teach_all, n, other)
        n *= 2
    far = swap_rows(lax.optimization_barrier((near, other))[0], GROUP)
    n = 2 * GROUP
    while n < n_rows:
        far = jnp.concatenate([far, swap_rows(jnp.concatenate([near, far], axis=0), n)], axis=0)
        n *= 2
    energy, sums = energy_call(teach_all.reshape(t, d), unit, total_k)
    sums = lax.optimization_barrier((total(sums), denom_near))[0]
    far_pairs = pairs_of(far)
    expo_far, denom_far, far_t, more_weight = student_call(far, far_pairs, unit, t, False)
    pairs = jnp.concatenate([near_pairs, far_pairs], axis=1)
    (sums,) = iterate_call(sums, energy, total_k)
    sums = lax.optimization_barrier((sums, far))[0]
    both, mean, scaled = iterate_call(total(sums), energy, total_k, (unit, denom_near, denom_far))
    both = total(both)
    students = (expo_near, expo_far, near_t, far_t, weight, more_weight)

    rows = d // n_rows
    chunks = CHUNKS // PARTS
    more = (pull, mean)
    pieces = []
    for first in range(0, CHUNKS, chunks):
        out = head_call(
            first, chunks, place, both, pairs, students, inv, scaled, v, factor, rows, more
        )
        if first == 0:
            body_rows, send, tail = out[GROUP:]
        more = (out[0],)
        arrived = []
        for n in range(1, GROUP):
            share = out[n]
            if pieces:
                share, pieces[-1][n - 1] = lax.optimization_barrier((share, pieces[-1][n - 1]))
            arrived.append(swap_rows(share, n))
        pieces.append(arrived)
    n = n_proto // 2
    while n >= 1:
        if n < n_proto // 2:
            height = body_rows.shape[0] // 2
            bit = (p // n) % 2
            send = lax.dynamic_slice_in_dim(body_rows, (1 - bit) * height, height, 0)
            body_rows = lax.dynamic_slice_in_dim(body_rows, bit * height, height, 0)
            send = jnp.concatenate([send, tail], axis=0)
        got = swap_proto(send, n)
        height = body_rows.shape[0]
        body_rows, tail = body_rows + got[:height], tail + got[height:]
        n //= 2
    terms = jnp.concatenate([body_rows, tail], axis=0)

    def block(n):
        return lax.dynamic_slice_in_dim(terms, (at ^ n) * s_dev, s_dev, 1)

    parts = [block(0)] + [swap_rows(block(n), n) for n in range(1, GROUP)]
    pieces[-1] = lax.optimization_barrier((pieces[-1], parts))[0]
    proto_grad = out[0]
    for part, arrived in enumerate(pieces):
        for n, got in enumerate(arrived, 1):
            start = (at ^ n) * kl + part * (kl // PARTS)
            proto_grad = lax.dynamic_update_slice(proto_grad, got.astype(F32), (0, start))
    own = lax.dynamic_slice_in_dim(both, t + at * s_dev, s_dev, 1)
    student_grad, loss = finish_call(t, place, both, own, own_pairs, student_features, parts, d // n_proto)
    return (proto_grad, student_grad.T, loss.reshape(s_dev))


def solution(mesh):
    return jax.shard_map(
        body,
        mesh=mesh,
        in_specs=(P("rows", None), P("rows", None), P(None, "proto"), P("rows")),
        out_specs=(P("rows", "proto"), P("rows", "proto"), P("rows")),
        check_vma=False,
    )
```

```python
import functools

import jax
import jax.numpy as jnp
from jax import lax
from jax.experimental import pallas as pl
from jax.experimental.pallas import tpu as pltpu
from jax.sharding import PartitionSpec as P

teacher_temp = 0.07
student_temp = 0.1
eps = 1e-06
LOG2E = 1.4426950408889634
GROUP = 4
CHUNKS = 4
SPLIT = 2
LIMIT = 44
SIZES = (5, 3)
F32 = jnp.float32
BF16 = jnp.bfloat16
NT = (((1,), (1,)), ((), ()))


def params(mib):
    return pltpu.CompilerParams(vmem_limit_bytes=mib * 1024 * 1024)


def vmem(count):
    return [pl.BlockSpec(memory_space=pltpu.VMEM)] * count


def anywhere(count):
    return [pl.BlockSpec(memory_space=pl.ANY)] * count


def grid_one(*shapes):
    return [pl.BlockSpec(shape, lambda i, n=len(shape): (0,) * n) for shape in shapes]


SMEM = pl.BlockSpec(memory_space=pltpu.SMEM)
DMA = pltpu.SemaphoreType.DMA
AHEAD = 4


def begin(chunks, fetch):
    for i in range(min(AHEAD, chunks)):
        for copy in fetch(i):
            copy.start()


def stream(chunks, fetch, work):
    @pl.loop(0, chunks)
    def _(i):
        @pl.when(i + AHEAD < chunks)
        def _():
            for copy in fetch(i + AHEAD):
                copy.start()

        for copy in fetch(i):
            copy.wait()
        work(i)


def to_column(row):
    return jnp.broadcast_to(row, (128, row.shape[1])).T


def lane_sums(x):
    total = x[:, :128]
    for at in range(128, x.shape[1], 128):
        total = total + x[:, at : at + 128]
    return total


def to_row(acc):
    return jnp.sum(acc.T, axis=0, keepdims=True)


def pick(column, pairs):
    t, n = column.shape[0], pairs.shape[1]
    out = []
    for at in range(0, n, 128):
        width = min(128, n - at)
        which = lax.broadcasted_iota(jnp.int32, (t, width), 0)
        hit = which == pairs[:, at : at + width]
        out.append(jnp.sum(jnp.where(hit, column[:, :width], 0.0), axis=0, keepdims=True))
    return jnp.concatenate(out, axis=1)


def prepare_kernel(teach_ref, stud_ref, pairs_ref, out_ref, digits):
    t, s = teach_ref.shape[0], stud_ref.shape[0]
    for ref, at, n in ((teach_ref, 0, t), (stud_ref, t, s)):
        x = ref[...].astype(F32)
        norm = jnp.sqrt(jnp.sum(x * x, axis=1, keepdims=True) + eps)
        out_ref[at : at + n, :] = (x / norm).astype(BF16)
    pairs = pairs_ref[...]
    high = lax.shift_right_logical(pairs, 6)
    row = lax.broadcasted_iota(jnp.int32, (16, s), 0)
    digits[...] = jnp.zeros_like(digits)
    digits[:, :s] = jnp.where(row == 0, high, jnp.where(row == 1, pairs - high * 64, 0)).astype(F32)
    out_ref[t + s :, :] = digits[...].astype(BF16)


def prepare_call(teach, stud, pairs):
    t, s, d = teach.shape[0], stud.shape[0], stud.shape[1]
    return pl.pallas_call(
        prepare_kernel,
        out_shape=jax.ShapeDtypeStruct((t + s + 16, d), BF16),
        grid=(1,),
        in_specs=grid_one((t, d), (s, d), (1, s)),
        out_specs=grid_one((t + s + 16, d))[0],
        scratch_shapes=[pltpu.VMEM((16, d), F32)],
        compiler_params=params(58),
        name="prepare",
    )(teach, stud, pairs)


def unit_kernel(place, v_hbm, unit_hbm, inv_ref, v, unit, sems_in, sems_out):
    chunks, _, width = v.shape

    def fetch(i):
        start = pl.multiple_of((place[0] * chunks + i) * width, width)
        return (pltpu.make_async_copy(v_hbm.at[:, pl.ds(start, width)], v.at[i], sems_in.at[i]),)

    def store(i):
        return pltpu.make_async_copy(unit.at[i], unit_hbm.at[i], sems_out.at[i])

    begin(chunks, fetch)

    def work(i):
        x = v[i].astype(F32)
        inv = lax.rsqrt(jnp.sum(x * x, axis=0, keepdims=True) + eps)
        unit[i] = (x * inv).astype(BF16)
        inv_ref[i] = inv
        store(i).start()

    stream(chunks, fetch, work)
    for i in range(chunks):
        store(i).wait()


def unit_call(place, v, kl):
    d = v.shape[0]
    shape = (CHUNKS, d, kl // CHUNKS)
    return pl.pallas_call(
        unit_kernel,
        out_shape=(
            jax.ShapeDtypeStruct(shape, BF16),
            jax.ShapeDtypeStruct((CHUNKS, 1, kl // CHUNKS), F32),
        ),
        in_specs=[SMEM] + anywhere(1),
        out_specs=tuple(anywhere(1) + vmem(1)),
        scratch_shapes=[pltpu.VMEM(shape, BF16), pltpu.VMEM(shape, BF16), DMA((CHUNKS,)), DMA((CHUNKS,))],
        cost_estimate=pl.CostEstimate(flops=4 * d * kl, bytes_accessed=4 * d * kl, transcendentals=kl),
        compiler_params=params(LIMIT),
        name="unit",
    )(place, v)


def energy_kernel(total_k, teach_ref, unit_hbm, energy_hbm, sum_ref, unit, energy, acc, sems_in, sems_out):
    chunks = unit.shape[0]

    def fetch(i):
        return (pltpu.make_async_copy(unit_hbm.at[i], unit.at[i], sems_in.at[i]),)

    def store(i):
        return pltpu.make_async_copy(energy.at[i], energy_hbm.at[i], sems_out.at[i])

    begin(chunks, fetch)
    acc[...] = jnp.zeros_like(acc)

    def work(i):
        dots = jnp.dot(teach_ref[...], unit[i], preferred_element_type=F32)
        e = jnp.exp2(dots * (LOG2E / teacher_temp))
        energy[i] = e.astype(BF16)
        store(i).start()
        col = 1.0 / (jnp.sum(e, axis=0, keepdims=True) * total_k)
        acc[...] += lane_sums(e * col)

    stream(chunks, fetch, work)
    sum_ref[...] = to_row(acc[...])
    for i in range(chunks):
        store(i).wait()


def energy_call(teach, unit, total_k):
    t, d = teach.shape
    chunks, _, width = unit.shape
    shape = (chunks, t, width)
    return pl.pallas_call(
        functools.partial(energy_kernel, float(total_k)),
        out_shape=(jax.ShapeDtypeStruct(shape, BF16), jax.ShapeDtypeStruct((1, t), F32)),
        in_specs=vmem(1) + anywhere(1),
        out_specs=tuple(anywhere(1) + vmem(1)),
        scratch_shapes=[
            pltpu.VMEM(unit.shape, BF16), pltpu.VMEM(shape, BF16), pltpu.VMEM((t, 128), F32),
            DMA((chunks,)), DMA((chunks,)),
        ],
        cost_estimate=pl.CostEstimate(
            flops=2 * t * d * chunks * width, bytes_accessed=4 * t * chunks * width, transcendentals=0
        ),
        compiler_params=params(LIMIT),
        name="energy",
    )(teach, unit)


def iterate_kernel(total_k, last, sum_in, energy_hbm, *refs):
    if last:
        near_ref, far_ref, sum_ref, scaled_hbm = refs[:4]
        acc, row, energy, sems_in, scaled, sems_out = refs[4:]
    else:
        sum_ref, acc, row, energy, sems_in = refs
    chunks, t, width = energy.shape

    def fetch(i):
        return (pltpu.make_async_copy(energy_hbm.at[i], energy.at[i], sems_in.at[i]),)

    def store(i):
        return pltpu.make_async_copy(scaled.at[i], scaled_hbm.at[i], sems_out.at[i])

    begin(chunks, fetch)
    row[...] = to_column(1.0 / (sum_in[...] * float(t)))
    acc[...] = jnp.zeros_like(acc)

    def work(i):
        scale = row[...]
        col = []
        for at in range(0, width, 128):
            mass = jnp.sum(energy[i, :, at : at + 128].astype(F32) * scale, axis=0, keepdims=True)
            col.append(1.0 / (mass * total_k))
        part = None
        for n, at in enumerate(range(0, width, 128)):
            x = energy[i, :, at : at + 128].astype(F32) * col[n]
            if last:
                scaled[i, :, at : at + 128] = x.astype(BF16)
            part = x if part is None else part + x
        acc[...] += part
        if last:
            store(i).start()

    stream(chunks, fetch, work)
    sum_ref[:, :t] = to_row(acc[...])
    if last:
        n = near_ref.shape[1]
        sum_ref[:, t : t + n] = near_ref[...]
        sum_ref[:, t + n :] = far_ref[...]
        for i in range(chunks):
            store(i).wait()


def iterate_call(sums, energy, total_k, more=()):
    chunks, t, width = energy.shape
    last = bool(more)
    out_shape = [jax.ShapeDtypeStruct((1, t), F32)]
    in_specs, out_specs = vmem(1) + anywhere(1), vmem(1)
    scratch = [
        pltpu.VMEM((t, 128), F32), pltpu.VMEM((t, 128), F32), pltpu.VMEM(energy.shape, BF16), DMA((chunks,))
    ]
    if last:
        near, far = more
        out_shape = [
            jax.ShapeDtypeStruct((1, t + near.shape[1] + far.shape[1]), F32),
            jax.ShapeDtypeStruct(energy.shape, BF16),
        ]
        in_specs, out_specs = in_specs + vmem(2), vmem(1) + anywhere(1)
        scratch += [pltpu.VMEM(energy.shape, BF16), DMA((chunks,))]
    return pl.pallas_call(
        functools.partial(iterate_kernel, float(total_k), last),
        out_shape=out_shape,
        in_specs=in_specs,
        out_specs=out_specs,
        scratch_shapes=scratch,
        cost_estimate=pl.CostEstimate(
            flops=4 * t * chunks * width, bytes_accessed=4 * t * chunks * width, transcendentals=0
        ),
        compiler_params=params(LIMIT),
        name="iterate_last" if last else "iterate",
    )(sums, energy, *more)


def student_kernel(block, near, rest_ref, pairs_ref, unit_hbm, expo_hbm, denom_ref, stud_t_ref, weight_ref, *refs):
    if near:
        pull_ref, pull, refs = refs[0], refs[-1], refs[1:-1]
        pull[...] = jnp.zeros_like(pull)
    unit, expo, acc, stud, sems_in, sems_out = refs
    chunks, s, width = expo.shape
    s_dev = s // rest_ref.shape[0]
    t = weight_ref.shape[1]

    def fetch(i):
        return (pltpu.make_async_copy(unit_hbm.at[i], unit.at[i], sems_in.at[i]),)

    def store(i):
        return pltpu.make_async_copy(expo.at[i], expo_hbm.at[i], sems_out.at[i])

    begin(chunks, fetch)
    acc[...] = jnp.zeros_like(acc)
    for i in range(rest_ref.shape[0]):
        stud[i * s_dev : (i + 1) * s_dev, :] = rest_ref[i, :s_dev, :]
    rows_t = stud[...].astype(F32).T.astype(BF16)
    stud_t_ref[...] = rows_t
    which = lax.broadcasted_iota(jnp.int32, (t, s), 0)
    onehot = (which == pairs_ref[...]).astype(F32).astype(BF16)
    weight_ref[...] = lax.dot_general(rows_t, onehot, NT, preferred_element_type=F32)

    def work(i):
        for at in range(0, s, block):
            logits = jnp.dot(stud[at : at + block, :], unit[i], preferred_element_type=F32)
            x = jnp.exp2(logits * (LOG2E / student_temp))
            expo[i, at : at + block, :] = x.astype(BF16)
            acc[at : at + block, :] += lane_sums(x)
        store(i).start()
        if near:
            pull[...] += lax.dot_general(expo[i], unit[i], NT, preferred_element_type=F32)

    stream(chunks, fetch, work)
    denom_ref[...] = to_row(acc[...])
    if near:
        pull_ref[...] = pull[...].T
    for i in range(chunks):
        store(i).wait()


def student_call(rest, pairs, unit, t, near):
    chunks, d, width = unit.shape
    s = rest.shape[0] * (rest.shape[1] - 16)
    shape = (chunks, s, width)
    out_shape = [
        jax.ShapeDtypeStruct(shape, BF16),
        jax.ShapeDtypeStruct((1, s), F32),
        jax.ShapeDtypeStruct((d, s), BF16),
        jax.ShapeDtypeStruct((d, t), F32),
    ]
    scratch = [
        pltpu.VMEM(unit.shape, BF16), pltpu.VMEM(shape, BF16), pltpu.VMEM((s, 128), F32),
        pltpu.VMEM((s, d), BF16), DMA((chunks,)), DMA((chunks,)),
    ]
    if near:
        out_shape += [jax.ShapeDtypeStruct((d, s), F32)]
        scratch += [pltpu.VMEM((s, d), F32)]
    return pl.pallas_call(
        functools.partial(student_kernel, 2 * (rest.shape[1] - 16), near),
        out_shape=out_shape,
        in_specs=vmem(2) + anywhere(1),
        out_specs=anywhere(1) + vmem(len(out_shape) - 1),
        scratch_shapes=scratch,
        cost_estimate=pl.CostEstimate(
            flops=4 * s * d * chunks * width, bytes_accessed=2 * s * chunks * width, transcendentals=0
        ),
        compiler_params=params(LIMIT),
        name="student_near" if near else "student_far",
    )(rest, pairs, unit)


def mean_kernel(pairs_ref, unit_hbm, scaled_hbm, mean_ref, unit, scaled, total, sems):
    chunks, t, width = scaled.shape

    def fetch(i):
        return (
            pltpu.make_async_copy(unit_hbm.at[i], unit.at[i], sems.at[i, 0]),
            pltpu.make_async_copy(scaled_hbm.at[i], scaled.at[i], sems.at[i, 1]),
        )

    begin(chunks, fetch)
    total[...] = jnp.zeros_like(total)

    def work(i):
        total[...] += lax.dot_general(unit[i], scaled[i], NT, preferred_element_type=F32)

    stream(chunks, fetch, work)
    pairs = pairs_ref[...]
    which = lax.broadcasted_iota(jnp.int32, (t, pairs.shape[1]), 0)
    mean_ref[...] = jnp.dot(
        total[...], (which == pairs).astype(F32), preferred_element_type=F32, precision=lax.Precision.HIGHEST
    )


def mean_call(pairs, unit, scaled):
    chunks, d, width = unit.shape
    t = scaled.shape[1]
    return pl.pallas_call(
        mean_kernel,
        out_shape=jax.ShapeDtypeStruct((d, pairs.shape[1]), F32),
        in_specs=vmem(1) + anywhere(2),
        out_specs=vmem(1)[0],
        scratch_shapes=[
            pltpu.VMEM(unit.shape, BF16), pltpu.VMEM(scaled.shape, BF16), pltpu.VMEM((d, t), F32), DMA((chunks, 2))
        ],
        cost_estimate=pl.CostEstimate(
            flops=6 * t * d * chunks * width, bytes_accessed=4 * d * chunks * width, transcendentals=0
        ),
        compiler_params=params(LIMIT),
        name="mean",
    )(pairs, unit, scaled)


def back_terms(factor, place, both_ref, pairs_ref, stud_t_ref, pull_ref, mean_ref, keep_ref, send_ref, tail_ref, back):
    d, n = pull_ref.shape
    t = both_ref.shape[1] - pairs_ref.shape[1]
    sums = both_ref[:, :t]
    denom = both_ref[:, t : t + n]
    row = 1.0 / (sums * float(t))
    pairs = pairs_ref[:, :n]
    mass = pick(to_column(row * sums * float(t)), pairs)
    target = mean_ref[...] * pick(to_column(row * float(t)), pairs)
    stud_t = stud_t_ref[...].astype(F32)
    terms = (pull_ref[...] * (mass / denom) - target) * factor
    back[...] = terms
    along = jnp.sum(stud_t * terms, axis=0, keepdims=True)
    cross = jnp.sum(stud_t * target, axis=0, keepdims=True) * (1.0 / student_temp)
    at = lax.broadcasted_iota(jnp.int32, (8, n), 0)
    tail = jnp.where(at == 0, along, jnp.where(at == 1, cross, 0.0))
    half = d // 2
    keep_ref[...] = back[pl.ds(pl.multiple_of(place[3] * half, half), half), :]
    send_ref[:half, :] = back[pl.ds(pl.multiple_of((1 - place[3]) * half, half), half), :]
    send_ref[half:, :] = tail
    tail_ref[...] = tail


def head_kernel(factor, first, place, both_ref, pairs_ref, near_ref, far_ref, weight_ref, more_weight_ref,
                inv_ref, near_hbm, far_hbm, scaled_hbm, v_hbm, *refs):
    if first == 0:
        pull_ref, mean_ref, own_hbm = refs[:3]
        sends, terms, refs = refs[3 : GROUP + 2], refs[GROUP + 2 : GROUP + 5], refs[GROUP + 5 :]
        back, refs = refs[-1], refs[:-1]
    else:
        own_hbm, sends, refs = refs[1], refs[2 : GROUP + 1], refs[GROUP + 1 :]
    lhs, lhs_teach, grad, expo, scaled, v, own, sems_in, sems_out = refs
    chunks, t, width = scaled.shape
    all_chunks = SPLIT * inv_ref.shape[0]
    n_near, n_far = near_ref.shape[1], far_ref.shape[1]
    rows = own.shape[1]

    def cut(ref, i):
        at = (first + i) // SPLIT
        return ref.at[at, :, pl.ds(pl.multiple_of((first + i - at * SPLIT) * width, width), width)]

    def start_of(i):
        return pl.multiple_of((place[0] * all_chunks + first + i) * width, width)

    def fetches(i):
        return (
            pltpu.make_async_copy(cut(near_hbm, i), expo.at[i, pl.ds(0, n_near), :], sems_in.at[i, 0]),
            pltpu.make_async_copy(cut(far_hbm, i), expo.at[i, pl.ds(n_near, n_far), :], sems_in.at[i, 3]),
            pltpu.make_async_copy(cut(scaled_hbm, i), scaled.at[i], sems_in.at[i, 1]),
            pltpu.make_async_copy(v_hbm.at[:, pl.ds(start_of(i), width)], v.at[i], sems_in.at[i, 2]),
        )

    def store(i):
        return pltpu.make_async_copy(own.at[i], own_hbm.at[:, pl.ds(start_of(i), width)], sems_out.at[i])

    begin(chunks, fetches)
    sums, denom = both_ref[:, :t], both_ref[:, t:]
    row = 1.0 / (sums * float(t))
    mass = pick(to_column(row * sums * float(t)), pairs_ref[...])
    scale = mass / denom * factor
    lhs[:, :n_near] = (near_ref[...].astype(F32) * scale[:, :n_near]).astype(BF16)
    lhs[:, n_near:] = (far_ref[...].astype(F32) * scale[:, n_near:]).astype(BF16)
    lhs_teach[...] = ((weight_ref[...] + more_weight_ref[...]) * (row * (-factor * t))).astype(BF16)
    if first == 0:
        back_terms(factor, place, both_ref, pairs_ref, near_ref, pull_ref, mean_ref, *terms, back)
    base = place[1] * (rows * GROUP)

    def part(n):
        start = pl.multiple_of(base + (place[0] ^ n) * rows, rows)
        return grad[pl.ds(start, rows), :]

    def work(i):
        head = jnp.dot(lhs[...], expo[i], preferred_element_type=F32)
        head = head + jnp.dot(lhs_teach[...], scaled[i], preferred_element_type=F32)
        inv = cut(inv_ref, i)[...]
        unit = v[i].astype(F32) * inv
        proj = jnp.sum(unit * head, axis=0, keepdims=True)
        grad[...] = (head - unit * proj) * inv
        own[i] = part(0)
        store(i).start()
        at = pl.ds(pl.multiple_of(i * width, width), width)
        for n, ref in enumerate(sends):
            ref[:, at] = part(n + 1).astype(BF16)

    stream(chunks, fetches, work)
    for i in range(chunks):
        store(i).wait()


def head_call(first, chunks, place, both, pairs, students, inv, scaled, v, factor, rows, more):
    near, far, near_t, far_t, weight, more_weight = students
    d, s = near_t.shape[0], pairs.shape[1]
    t, width = scaled.shape[1], scaled.shape[2] // SPLIT
    kl = chunks * width
    out_shape = [jax.ShapeDtypeStruct((rows, v.shape[1]), F32)] + [jax.ShapeDtypeStruct((rows, kl), BF16)] * (GROUP - 1)
    out_specs = anywhere(1) + vmem(GROUP - 1)
    scratch = [
        pltpu.VMEM((d, s), BF16), pltpu.VMEM((d, t), BF16), pltpu.VMEM((d, width), F32),
        pltpu.VMEM((chunks, s, width), BF16), pltpu.VMEM((chunks, t, width), BF16),
        pltpu.VMEM((chunks, d, width), BF16), pltpu.VMEM((chunks, rows, width), F32),
        DMA((chunks, 4)), DMA((chunks,)),
    ]
    if first == 0:
        n = more[0].shape[1]
        out_shape += [
            jax.ShapeDtypeStruct((d // 2, n), F32),
            jax.ShapeDtypeStruct((d // 2 + 8, n), F32),
            jax.ShapeDtypeStruct((8, n), F32),
        ]
        out_specs += vmem(3)
        scratch += [pltpu.VMEM((d, n), F32)]
    return pl.pallas_call(
        functools.partial(head_kernel, factor, first),
        out_shape=out_shape,
        in_specs=[SMEM] + vmem(7) + anywhere(4) + (vmem(2) if first == 0 else anywhere(1)),
        out_specs=out_specs,
        scratch_shapes=scratch,
        input_output_aliases={} if first == 0 else {12: 0},
        cost_estimate=pl.CostEstimate(
            flops=4 * (s + t) * d * kl, bytes_accessed=2 * (s + t + d) * kl, transcendentals=0
        ),
        compiler_params=params(LIMIT),
        name="head",
    )(place, both, pairs, near_t, far_t, weight, more_weight, inv, near, far, scaled, v, *more)


def place_kernel(first, place, *refs):
    arrived, refs = refs[: GROUP - 1], refs[GROUP:]
    out_hbm, got, wide, sems_in, sems_out = refs
    width = wide.shape[2]
    count = out_hbm.shape[1] // GROUP

    def fetch(n):
        return pltpu.make_async_copy(arrived[n], got.at[n], sems_in.at[n])

    def store(n):
        start = pl.multiple_of((place[0] ^ (n + 1)) * count + first, 128)
        return pltpu.make_async_copy(wide.at[n], out_hbm.at[:, pl.ds(start, width)], sems_out.at[n])

    for n in range(GROUP - 1):
        fetch(n).start()
    for n in range(GROUP - 1):
        fetch(n).wait()
        wide[n] = got[n].astype(F32)
        store(n).start()
    for n in range(GROUP - 1):
        store(n).wait()


def place_call(first, place, arrived, out):
    rows, width = arrived[0].shape
    return pl.pallas_call(
        functools.partial(place_kernel, first),
        out_shape=jax.ShapeDtypeStruct(out.shape, F32),
        in_specs=[SMEM] + anywhere(GROUP),
        out_specs=anywhere(1)[0],
        scratch_shapes=[
            pltpu.VMEM((GROUP - 1, rows, width), BF16), pltpu.VMEM((GROUP - 1, rows, width), F32),
            DMA((GROUP - 1,)), DMA((GROUP - 1,)),
        ],
        input_output_aliases={GROUP: 0},
        cost_estimate=pl.CostEstimate(flops=0, bytes_accessed=18 * rows * width, transcendentals=0),
        compiler_params=params(LIMIT),
        name="place",
    )(place, *arrived, out)


def finish_kernel(t, place, both_ref, denom_ref, pairs_ref, stud_ref, *refs):
    terms, (grad_ref, loss_ref, unit) = refs[:GROUP], refs[GROUP:]
    total = (terms[0][...] + terms[1][...]) + (terms[2][...] + terms[3][...])
    share = grad_ref.shape[0]
    x = stud_ref[...].astype(F32).T
    norm = jnp.sqrt(jnp.sum(x * x, axis=0, keepdims=True) + eps)
    unit[...] = x / norm
    part = unit[pl.ds(pl.multiple_of(place[2] * share, share), share), :]
    along, cross = total[share : share + 1, :], total[share + 1 : share + 2, :]
    grad_ref[...] = (total[:share, :] - part * along) / norm
    sums = both_ref[:, :t]
    mass = pick(to_column(1.0 / (sums * float(t)) * sums * float(t)), pairs_ref[...])
    loss_ref[...] = jnp.log(denom_ref[...]) * mass - cross


def finish_call(t, place, both, denom, pairs, stud, terms, share):
    s, d = stud.shape
    return pl.pallas_call(
        functools.partial(finish_kernel, t),
        out_shape=(jax.ShapeDtypeStruct((share, s), F32), jax.ShapeDtypeStruct((1, s), F32)),
        in_specs=[SMEM] + vmem(4 + GROUP),
        out_specs=tuple(vmem(2)),
        scratch_shapes=[pltpu.VMEM((d, s), F32)],
        compiler_params=params(8),
        name="finish",
    )(place, both, denom, pairs, stud, *terms)


def body(teacher_features, student_features, v, pairing):
    n_rows, n_proto = lax.axis_size("rows"), lax.axis_size("proto")
    r, p = lax.axis_index("rows"), lax.axis_index("proto")
    d, local_k = v.shape
    total_k = local_k * n_proto
    kl = local_k // GROUP
    t_dev, s_dev = teacher_features.shape[0], student_features.shape[0]
    t, s = t_dev * n_rows, s_dev * n_rows
    at, group = r % GROUP, r // GROUP
    top = (p * 2) // n_proto
    place = jnp.stack([at, group, p, top]).astype(jnp.int32)
    factor = total_k / 64.0 / student_temp

    def swap_rows(x, n):
        return lax.ppermute(x, "rows", [(j, j ^ n) for j in range(n_rows)])

    def swap_proto(x, n):
        return lax.ppermute(x, "proto", [(j, j ^ n) for j in range(n_proto)])

    def over(swap, size, x):
        n = 1
        while n < size:
            x = (x + swap(x, n)) + (swap(x, 2 * n) + swap(x, 3 * n))
            n *= 4
        return x

    def over_proto(x):
        return over(swap_proto, n_proto, x)

    def over_group(x):
        return over(swap_rows, GROUP, x)

    def total(x):
        return over_group(over_proto(x))

    def join(x, n, other=None):
        other = swap_rows(x, n) if other is None else other
        low = (r // n) % 2 == 0
        return jnp.concatenate([jnp.where(low, x, other), jnp.where(low, other, x)], axis=0)

    own_pairs = pairing.reshape(1, s_dev)
    unit, inv = unit_call(place, v, kl)
    packed = prepare_call(teacher_features, student_features, own_pairs)
    blocks = [packed] + [swap_rows(packed, n) for n in range(1, GROUP)]
    blocks[-1], unit, inv = lax.optimization_barrier((blocks[-1], unit, inv))
    for n in (1, 2):
        low = (at // n) % 2 == 0
        blocks = [jnp.where(low, blocks[j], blocks[j ^ n]) for j in range(GROUP)]
    packed = jnp.stack(blocks)
    teach_all, near = packed[:, :t_dev], packed[:, t_dev:]

    def pairs_of(rest):
        digits = rest[:, s_dev : s_dev + 2, :s_dev].astype(F32)
        return (digits[:, 0] * 64.0 + digits[:, 1]).astype(jnp.int32).reshape(1, -1)

    near_pairs = pairs_of(near)
    n = GROUP
    while n < n_rows:
        other = swap_rows(teach_all, n)
        teach_all = join(teach_all, n, other)
        n *= 2
    far = swap_rows(lax.optimization_barrier((near, other))[0], GROUP)
    n = 2 * GROUP
    while n < n_rows:
        far = jnp.concatenate([far, swap_rows(jnp.concatenate([near, far], axis=0), n)], axis=0)
        n *= 2
    energy, sums = energy_call(teach_all.reshape(t, d), unit, total_k)
    sums = over_proto(sums)
    near = lax.optimization_barrier((near, sums))[0]
    expo_near, denom_near, near_t, weight, pull = student_call(near, near_pairs, unit, t, True)
    sums = lax.optimization_barrier((over_group(sums), denom_near))[0]
    far_pairs = pairs_of(far)
    expo_far, denom_far, far_t, more_weight = student_call(far, far_pairs, unit, t, False)
    pairs = jnp.concatenate([near_pairs, far_pairs], axis=1)
    (sums,) = iterate_call(sums, energy, total_k)
    sums = lax.optimization_barrier((sums, far))[0]
    both, scaled = iterate_call(total(sums), energy, total_k, (denom_near, denom_far))
    mean = mean_call(near_pairs, unit, scaled)
    both = total(both)
    students = (expo_near, expo_far, near_t, far_t, weight, more_weight)

    rows = d // n_rows
    width = kl // (CHUNKS * SPLIT)
    offsets = [sum(SIZES[:n]) for n in range(len(SIZES))]
    more = (pull, mean)
    pieces = []
    for first, chunks in zip(offsets, SIZES):
        out = head_call(
            first, chunks, place, both, pairs, students, inv, scaled, v, factor, rows, more
        )
        if first == 0:
            body_rows, send, tail = out[GROUP:]
        more = (out[0],)
        arrived = []
        for n in range(1, GROUP):
            share = out[n]
            if pieces and n == GROUP - 1:
                share = lax.optimization_barrier((share, pieces[-1]))[0]
            arrived.append(swap_rows(share, n))
        pieces.append(arrived)
    proto_grad = out[0]
    for part, arrived in enumerate(pieces[:-1]):
        proto_grad = place_call(offsets[part] * width, place, arrived, proto_grad)
    n = n_proto // 2
    while n >= 1:
        if n < n_proto // 2:
            height = body_rows.shape[0] // 2
            bit = (p // n) % 2
            send = lax.dynamic_slice_in_dim(body_rows, (1 - bit) * height, height, 0)
            body_rows = lax.dynamic_slice_in_dim(body_rows, bit * height, height, 0)
            send = jnp.concatenate([send, tail], axis=0)
        got = lax.optimization_barrier((swap_proto(send, n), out[1] if n == n_proto // 2 else proto_grad))[0]
        height = body_rows.shape[0]
        body_rows, tail = body_rows + got[:height], tail + got[height:]
        n //= 2
    terms = jnp.concatenate([body_rows, tail], axis=0)

    def block(n):
        return lax.dynamic_slice_in_dim(terms, (at ^ n) * s_dev, s_dev, 1)

    parts = [block(0)] + [swap_rows(block(n), n) for n in range(1, GROUP)]
    proto_grad = place_call(offsets[-1] * width, place, pieces[-1], proto_grad)
    own = lax.dynamic_slice_in_dim(both, t + at * s_dev, s_dev, 1)
    student_grad, loss = finish_call(t, place, both, own, own_pairs, student_features, parts, d // n_proto)
    return (proto_grad, student_grad.T, loss.reshape(s_dev))


def solution(mesh):
    return jax.shard_map(
        body,
        mesh=mesh,
        in_specs=(P("rows", None), P("rows", None), P(None, "proto"), P("rows")),
        out_specs=(P("rows", "proto"), P("rows", "proto"), P("rows")),
        check_vma=False,
    )
```

```python
import functools

import jax
import jax.numpy as jnp
from jax import lax
from jax.experimental import pallas as pl
from jax.experimental.pallas import tpu as pltpu
from jax.sharding import PartitionSpec as P

teacher_temp = 0.07
student_temp = 0.1
eps = 1e-06
LOG2E = 1.4426950408889634
GROUP = 4
CHUNKS = 4
SPLIT = 2
LIMIT = 44
SIZES = (5, 3)
F32 = jnp.float32
BF16 = jnp.bfloat16
NT = (((1,), (1,)), ((), ()))


def params(mib):
    return pltpu.CompilerParams(vmem_limit_bytes=mib * 1024 * 1024)


def vmem(count):
    return [pl.BlockSpec(memory_space=pltpu.VMEM)] * count


def anywhere(count):
    return [pl.BlockSpec(memory_space=pl.ANY)] * count


def grid_one(*shapes):
    return [pl.BlockSpec(shape, lambda i, n=len(shape): (0,) * n) for shape in shapes]


SMEM = pl.BlockSpec(memory_space=pltpu.SMEM)
DMA = pltpu.SemaphoreType.DMA
AHEAD = 4


def begin(chunks, fetch):
    for i in range(min(AHEAD, chunks)):
        for copy in fetch(i):
            copy.start()


def stream(chunks, fetch, work):
    @pl.loop(0, chunks)
    def _(i):
        @pl.when(i + AHEAD < chunks)
        def _():
            for copy in fetch(i + AHEAD):
                copy.start()

        for copy in fetch(i):
            copy.wait()
        work(i)


def to_column(row):
    return jnp.broadcast_to(row, (128, row.shape[1])).T


def lane_sums(x):
    total = x[:, :128]
    for at in range(128, x.shape[1], 128):
        total = total + x[:, at : at + 128]
    return total


def to_row(acc):
    return jnp.sum(acc.T, axis=0, keepdims=True)


def pick(column, pairs):
    t, n = column.shape[0], pairs.shape[1]
    out = []
    for at in range(0, n, 128):
        width = min(128, n - at)
        which = lax.broadcasted_iota(jnp.int32, (t, width), 0)
        hit = which == pairs[:, at : at + width]
        out.append(jnp.sum(jnp.where(hit, column[:, :width], 0.0), axis=0, keepdims=True))
    return jnp.concatenate(out, axis=1)


def prepare_kernel(teach_ref, stud_ref, pairs_ref, out_ref, digits):
    t, s = teach_ref.shape[0], stud_ref.shape[0]
    for ref, at, n in ((teach_ref, 0, t), (stud_ref, t, s)):
        x = ref[...].astype(F32)
        norm = jnp.sqrt(jnp.sum(x * x, axis=1, keepdims=True) + eps)
        out_ref[at : at + n, :] = (x / norm).astype(BF16)
    pairs = pairs_ref[...]
    high = lax.shift_right_logical(pairs, 6)
    row = lax.broadcasted_iota(jnp.int32, (16, s), 0)
    digits[...] = jnp.zeros_like(digits)
    digits[:, :s] = jnp.where(row == 0, high, jnp.where(row == 1, pairs - high * 64, 0)).astype(F32)
    out_ref[t + s :, :] = digits[...].astype(BF16)


def prepare_call(teach, stud, pairs):
    t, s, d = teach.shape[0], stud.shape[0], stud.shape[1]
    return pl.pallas_call(
        prepare_kernel,
        out_shape=jax.ShapeDtypeStruct((t + s + 16, d), BF16),
        grid=(1,),
        in_specs=grid_one((t, d), (s, d), (1, s)),
        out_specs=grid_one((t + s + 16, d))[0],
        scratch_shapes=[pltpu.VMEM((16, d), F32)],
        compiler_params=params(58),
        name="prepare",
    )(teach, stud, pairs)


def unit_kernel(place, v_hbm, unit_hbm, inv_ref, v, unit, sems_in, sems_out):
    chunks, _, width = v.shape

    def fetch(i):
        start = pl.multiple_of((place[0] * chunks + i) * width, width)
        return (pltpu.make_async_copy(v_hbm.at[:, pl.ds(start, width)], v.at[i], sems_in.at[i]),)

    def store(i):
        return pltpu.make_async_copy(unit.at[i], unit_hbm.at[i], sems_out.at[i])

    begin(chunks, fetch)

    def work(i):
        x = v[i].astype(F32)
        inv = lax.rsqrt(jnp.sum(x * x, axis=0, keepdims=True) + eps)
        unit[i] = (x * inv).astype(BF16)
        inv_ref[i] = inv
        store(i).start()

    stream(chunks, fetch, work)
    for i in range(chunks):
        store(i).wait()


def unit_call(place, v, kl):
    d = v.shape[0]
    shape = (CHUNKS, d, kl // CHUNKS)
    return pl.pallas_call(
        unit_kernel,
        out_shape=(
            jax.ShapeDtypeStruct(shape, BF16),
            jax.ShapeDtypeStruct((CHUNKS, 1, kl // CHUNKS), F32),
        ),
        in_specs=[SMEM] + anywhere(1),
        out_specs=tuple(anywhere(1) + vmem(1)),
        scratch_shapes=[pltpu.VMEM(shape, BF16), pltpu.VMEM(shape, BF16), DMA((CHUNKS,)), DMA((CHUNKS,))],
        cost_estimate=pl.CostEstimate(flops=4 * d * kl, bytes_accessed=4 * d * kl, transcendentals=kl),
        compiler_params=params(LIMIT),
        name="unit",
    )(place, v)


def energy_kernel(total_k, teach_ref, unit_hbm, energy_hbm, sum_ref, unit, energy, acc, sems_in, sems_out):
    chunks = unit.shape[0]

    def fetch(i):
        return (pltpu.make_async_copy(unit_hbm.at[i], unit.at[i], sems_in.at[i]),)

    def store(i):
        return pltpu.make_async_copy(energy.at[i], energy_hbm.at[i], sems_out.at[i])

    begin(chunks, fetch)
    acc[...] = jnp.zeros_like(acc)

    def work(i):
        dots = jnp.dot(teach_ref[...], unit[i], preferred_element_type=F32)
        e = jnp.exp2(dots * (LOG2E / teacher_temp))
        energy[i] = e.astype(BF16)
        store(i).start()
        col = 1.0 / (jnp.sum(e, axis=0, keepdims=True) * total_k)
        acc[...] += lane_sums(e * col)

    stream(chunks, fetch, work)
    sum_ref[...] = to_row(acc[...])
    for i in range(chunks):
        store(i).wait()


def energy_call(teach, unit, total_k):
    t, d = teach.shape
    chunks, _, width = unit.shape
    shape = (chunks, t, width)
    return pl.pallas_call(
        functools.partial(energy_kernel, float(total_k)),
        out_shape=(jax.ShapeDtypeStruct(shape, BF16), jax.ShapeDtypeStruct((1, t), F32)),
        in_specs=vmem(1) + anywhere(1),
        out_specs=tuple(anywhere(1) + vmem(1)),
        scratch_shapes=[
            pltpu.VMEM(unit.shape, BF16), pltpu.VMEM(shape, BF16), pltpu.VMEM((t, 128), F32),
            DMA((chunks,)), DMA((chunks,)),
        ],
        cost_estimate=pl.CostEstimate(
            flops=2 * t * d * chunks * width, bytes_accessed=4 * t * chunks * width, transcendentals=0
        ),
        compiler_params=params(52),
        name="energy",
    )(teach, unit)


def iterate_kernel(total_k, last, sum_in, energy_hbm, *refs):
    if last:
        near_ref, far_ref, sum_ref, scaled_hbm = refs[:4]
        acc, row, energy, sems_in, scaled, sems_out = refs[4:]
    else:
        sum_ref, acc, row, energy, sems_in = refs
    chunks, t, width = energy.shape

    def fetch(i):
        return (pltpu.make_async_copy(energy_hbm.at[i], energy.at[i], sems_in.at[i]),)

    def store(i):
        return pltpu.make_async_copy(scaled.at[i], scaled_hbm.at[i], sems_out.at[i])

    begin(chunks, fetch)
    row[...] = to_column(1.0 / (sum_in[...] * float(t)))
    acc[...] = jnp.zeros_like(acc)

    def work(i):
        scale = row[...]
        col = []
        for at in range(0, width, 128):
            mass = jnp.sum(energy[i, :, at : at + 128].astype(F32) * scale, axis=0, keepdims=True)
            col.append(1.0 / (mass * total_k))
        part = None
        for n, at in enumerate(range(0, width, 128)):
            x = energy[i, :, at : at + 128].astype(F32) * col[n]
            if last:
                scaled[i, :, at : at + 128] = x.astype(BF16)
            part = x if part is None else part + x
        acc[...] += part
        if last:
            store(i).start()

    stream(chunks, fetch, work)
    sum_ref[:, :t] = to_row(acc[...])
    if last:
        n = near_ref.shape[1]
        sum_ref[:, t : t + n] = near_ref[...]
        sum_ref[:, t + n :] = far_ref[...]
        for i in range(chunks):
            store(i).wait()


def iterate_call(sums, energy, total_k, more=()):
    chunks, t, width = energy.shape
    last = bool(more)
    out_shape = [jax.ShapeDtypeStruct((1, t), F32)]
    in_specs, out_specs = vmem(1) + anywhere(1), vmem(1)
    scratch = [
        pltpu.VMEM((t, 128), F32), pltpu.VMEM((t, 128), F32), pltpu.VMEM(energy.shape, BF16), DMA((chunks,))
    ]
    if last:
        near, far = more
        out_shape = [
            jax.ShapeDtypeStruct((1, t + near.shape[1] + far.shape[1]), F32),
            jax.ShapeDtypeStruct(energy.shape, BF16),
        ]
        in_specs, out_specs = in_specs + vmem(2), vmem(1) + anywhere(1)
        scratch += [pltpu.VMEM(energy.shape, BF16), DMA((chunks,))]
    return pl.pallas_call(
        functools.partial(iterate_kernel, float(total_k), last),
        out_shape=out_shape,
        in_specs=in_specs,
        out_specs=out_specs,
        scratch_shapes=scratch,
        cost_estimate=pl.CostEstimate(
            flops=4 * t * chunks * width, bytes_accessed=4 * t * chunks * width, transcendentals=0
        ),
        compiler_params=params(LIMIT),
        name="iterate_last" if last else "iterate",
    )(sums, energy, *more)


def student_kernel(block, near, rest_ref, pairs_ref, unit_hbm, expo_hbm, denom_ref, stud_t_ref, weight_ref, *refs):
    if near:
        pull_ref, pull, refs = refs[0], refs[-1], refs[1:-1]
        pull[...] = jnp.zeros_like(pull)
    unit, expo, acc, stud, sems_in, sems_out = refs
    chunks, s, width = expo.shape
    s_dev = s // rest_ref.shape[0]
    t = weight_ref.shape[1]

    def fetch(i):
        return (pltpu.make_async_copy(unit_hbm.at[i], unit.at[i], sems_in.at[i]),)

    def store(i):
        return pltpu.make_async_copy(expo.at[i], expo_hbm.at[i], sems_out.at[i])

    begin(chunks, fetch)
    acc[...] = jnp.zeros_like(acc)
    for i in range(rest_ref.shape[0]):
        stud[i * s_dev : (i + 1) * s_dev, :] = rest_ref[i, :s_dev, :]
    rows_t = stud[...].astype(F32).T.astype(BF16)
    stud_t_ref[...] = rows_t
    which = lax.broadcasted_iota(jnp.int32, (t, s), 0)
    onehot = (which == pairs_ref[...]).astype(F32).astype(BF16)
    weight_ref[...] = lax.dot_general(rows_t, onehot, NT, preferred_element_type=F32)

    def work(i):
        for at in range(0, s, block):
            logits = jnp.dot(stud[at : at + block, :], unit[i], preferred_element_type=F32)
            x = jnp.exp2(logits * (LOG2E / student_temp))
            expo[i, at : at + block, :] = x.astype(BF16)
            acc[at : at + block, :] += lane_sums(x)
        store(i).start()
        if near:
            pull[...] += lax.dot_general(expo[i], unit[i], NT, preferred_element_type=F32)

    stream(chunks, fetch, work)
    denom_ref[...] = to_row(acc[...])
    if near:
        pull_ref[...] = pull[...].T
    for i in range(chunks):
        store(i).wait()


def student_call(rest, pairs, unit, t, near):
    chunks, d, width = unit.shape
    s = rest.shape[0] * (rest.shape[1] - 16)
    shape = (chunks, s, width)
    out_shape = [
        jax.ShapeDtypeStruct(shape, BF16),
        jax.ShapeDtypeStruct((1, s), F32),
        jax.ShapeDtypeStruct((d, s), BF16),
        jax.ShapeDtypeStruct((d, t), F32),
    ]
    scratch = [
        pltpu.VMEM(unit.shape, BF16), pltpu.VMEM(shape, BF16), pltpu.VMEM((s, 128), F32),
        pltpu.VMEM((s, d), BF16), DMA((chunks,)), DMA((chunks,)),
    ]
    if near:
        out_shape += [jax.ShapeDtypeStruct((d, s), F32)]
        scratch += [pltpu.VMEM((s, d), F32)]
    return pl.pallas_call(
        functools.partial(student_kernel, 2 * (rest.shape[1] - 16), near),
        out_shape=out_shape,
        in_specs=vmem(2) + anywhere(1),
        out_specs=anywhere(1) + vmem(len(out_shape) - 1),
        scratch_shapes=scratch,
        cost_estimate=pl.CostEstimate(
            flops=4 * s * d * chunks * width, bytes_accessed=2 * s * chunks * width, transcendentals=0
        ),
        compiler_params=params(52),
        name="student_near" if near else "student_far",
    )(rest, pairs, unit)


def mean_kernel(pairs_ref, unit_hbm, scaled_hbm, mean_ref, unit, scaled, total, sems):
    chunks, t, width = scaled.shape

    def fetch(i):
        return (
            pltpu.make_async_copy(unit_hbm.at[i], unit.at[i], sems.at[i, 0]),
            pltpu.make_async_copy(scaled_hbm.at[i], scaled.at[i], sems.at[i, 1]),
        )

    begin(chunks, fetch)
    total[...] = jnp.zeros_like(total)

    def work(i):
        total[...] += lax.dot_general(unit[i], scaled[i], NT, preferred_element_type=F32)

    stream(chunks, fetch, work)
    pairs = pairs_ref[...]
    which = lax.broadcasted_iota(jnp.int32, (t, pairs.shape[1]), 0)
    mean_ref[...] = jnp.dot(
        total[...], (which == pairs).astype(F32), preferred_element_type=F32, precision=lax.Precision.HIGHEST
    )


def mean_call(pairs, unit, scaled):
    chunks, d, width = unit.shape
    t = scaled.shape[1]
    return pl.pallas_call(
        mean_kernel,
        out_shape=jax.ShapeDtypeStruct((d, pairs.shape[1]), F32),
        in_specs=vmem(1) + anywhere(2),
        out_specs=vmem(1)[0],
        scratch_shapes=[
            pltpu.VMEM(unit.shape, BF16), pltpu.VMEM(scaled.shape, BF16), pltpu.VMEM((d, t), F32), DMA((chunks, 2))
        ],
        cost_estimate=pl.CostEstimate(
            flops=6 * t * d * chunks * width, bytes_accessed=4 * d * chunks * width, transcendentals=0
        ),
        compiler_params=params(LIMIT),
        name="mean",
    )(pairs, unit, scaled)


def back_terms(factor, place, both_ref, pairs_ref, stud_t_ref, pull_ref, mean_ref, keep_ref, send_ref, tail_ref, back):
    d, n = pull_ref.shape
    t = both_ref.shape[1] - pairs_ref.shape[1]
    sums = both_ref[:, :t]
    denom = both_ref[:, t : t + n]
    row = 1.0 / (sums * float(t))
    pairs = pairs_ref[:, :n]
    mass = pick(to_column(row * sums * float(t)), pairs)
    target = mean_ref[...] * pick(to_column(row * float(t)), pairs)
    stud_t = stud_t_ref[...].astype(F32)
    terms = (pull_ref[...] * (mass / denom) - target) * factor
    back[...] = terms
    along = jnp.sum(stud_t * terms, axis=0, keepdims=True)
    cross = jnp.sum(stud_t * target, axis=0, keepdims=True) * (1.0 / student_temp)
    at = lax.broadcasted_iota(jnp.int32, (8, n), 0)
    tail = jnp.where(at == 0, along, jnp.where(at == 1, cross, 0.0))
    half = d // 2
    keep_ref[...] = back[pl.ds(pl.multiple_of(place[3] * half, half), half), :]
    send_ref[:half, :] = back[pl.ds(pl.multiple_of((1 - place[3]) * half, half), half), :]
    send_ref[half:, :] = tail
    tail_ref[...] = tail


def head_kernel(factor, first, place, both_ref, pairs_ref, near_ref, far_ref, weight_ref, more_weight_ref,
                inv_ref, near_hbm, far_hbm, scaled_hbm, v_hbm, *refs):
    if first == 0:
        pull_ref, mean_ref, own_hbm = refs[:3]
        sends, terms, refs = refs[3 : GROUP + 2], refs[GROUP + 2 : GROUP + 5], refs[GROUP + 5 :]
        back, refs = refs[-1], refs[:-1]
    else:
        own_hbm, sends, refs = refs[1], refs[2 : GROUP + 1], refs[GROUP + 1 :]
    lhs, lhs_teach, grad, expo, scaled, v, own, sems_in, sems_out = refs
    chunks, t, width = scaled.shape
    all_chunks = SPLIT * inv_ref.shape[0]
    n_near, n_far = near_ref.shape[1], far_ref.shape[1]
    rows = own.shape[1]

    def cut(ref, i):
        at = (first + i) // SPLIT
        return ref.at[at, :, pl.ds(pl.multiple_of((first + i - at * SPLIT) * width, width), width)]

    def start_of(i):
        return pl.multiple_of((place[0] * all_chunks + first + i) * width, width)

    def fetches(i):
        return (
            pltpu.make_async_copy(cut(near_hbm, i), expo.at[i, pl.ds(0, n_near), :], sems_in.at[i, 0]),
            pltpu.make_async_copy(cut(far_hbm, i), expo.at[i, pl.ds(n_near, n_far), :], sems_in.at[i, 3]),
            pltpu.make_async_copy(cut(scaled_hbm, i), scaled.at[i], sems_in.at[i, 1]),
            pltpu.make_async_copy(v_hbm.at[:, pl.ds(start_of(i), width)], v.at[i], sems_in.at[i, 2]),
        )

    def store(i):
        return pltpu.make_async_copy(own.at[i], own_hbm.at[:, pl.ds(start_of(i), width)], sems_out.at[i])

    begin(chunks, fetches)
    sums, denom = both_ref[:, :t], both_ref[:, t:]
    row = 1.0 / (sums * float(t))
    mass = pick(to_column(row * sums * float(t)), pairs_ref[...])
    scale = mass / denom * factor
    lhs[:, :n_near] = (near_ref[...].astype(F32) * scale[:, :n_near]).astype(BF16)
    lhs[:, n_near:] = (far_ref[...].astype(F32) * scale[:, n_near:]).astype(BF16)
    lhs_teach[...] = ((weight_ref[...] + more_weight_ref[...]) * (row * (-factor * t))).astype(BF16)
    if first == 0:
        back_terms(factor, place, both_ref, pairs_ref, near_ref, pull_ref, mean_ref, *terms, back)
    base = place[1] * (rows * GROUP)

    def part(n):
        start = pl.multiple_of(base + (place[0] ^ n) * rows, rows)
        return grad[pl.ds(start, rows), :]

    def work(i):
        head = jnp.dot(lhs[...], expo[i], preferred_element_type=F32)
        head = head + jnp.dot(lhs_teach[...], scaled[i], preferred_element_type=F32)
        inv = cut(inv_ref, i)[...]
        unit = v[i].astype(F32) * inv
        proj = jnp.sum(unit * head, axis=0, keepdims=True)
        grad[...] = (head - unit * proj) * inv
        own[i] = part(0)
        store(i).start()
        at = pl.ds(pl.multiple_of(i * width, width), width)
        for n, ref in enumerate(sends):
            ref[:, at] = part(n + 1).astype(BF16)

    stream(chunks, fetches, work)
    for i in range(chunks):
        store(i).wait()


def head_call(first, chunks, place, both, pairs, students, inv, scaled, v, factor, rows, more):
    near, far, near_t, far_t, weight, more_weight = students
    d, s = near_t.shape[0], pairs.shape[1]
    t, width = scaled.shape[1], scaled.shape[2] // SPLIT
    kl = chunks * width
    out_shape = [jax.ShapeDtypeStruct((rows, v.shape[1]), F32)] + [jax.ShapeDtypeStruct((rows, kl), BF16)] * (GROUP - 1)
    out_specs = anywhere(1) + vmem(GROUP - 1)
    scratch = [
        pltpu.VMEM((d, s), BF16), pltpu.VMEM((d, t), BF16), pltpu.VMEM((d, width), F32),
        pltpu.VMEM((chunks, s, width), BF16), pltpu.VMEM((chunks, t, width), BF16),
        pltpu.VMEM((chunks, d, width), BF16), pltpu.VMEM((chunks, rows, width), F32),
        DMA((chunks, 4)), DMA((chunks,)),
    ]
    if first == 0:
        n = more[0].shape[1]
        out_shape += [
            jax.ShapeDtypeStruct((d // 2, n), F32),
            jax.ShapeDtypeStruct((d // 2 + 8, n), F32),
            jax.ShapeDtypeStruct((8, n), F32),
        ]
        out_specs += vmem(3)
        scratch += [pltpu.VMEM((d, n), F32)]
    return pl.pallas_call(
        functools.partial(head_kernel, factor, first),
        out_shape=out_shape,
        in_specs=[SMEM] + vmem(7) + anywhere(4) + (vmem(2) if first == 0 else anywhere(1)),
        out_specs=out_specs,
        scratch_shapes=scratch,
        input_output_aliases={} if first == 0 else {12: 0},
        cost_estimate=pl.CostEstimate(
            flops=4 * (s + t) * d * kl, bytes_accessed=2 * (s + t + d) * kl, transcendentals=0
        ),
        compiler_params=params(LIMIT),
        name="head",
    )(place, both, pairs, near_t, far_t, weight, more_weight, inv, near, far, scaled, v, *more)


def place_kernel(first, place, *refs):
    arrived, refs = refs[: GROUP - 1], refs[GROUP:]
    out_hbm, got, wide, sems_in, sems_out = refs
    width = wide.shape[2]
    count = out_hbm.shape[1] // GROUP

    def fetch(n):
        return pltpu.make_async_copy(arrived[n], got.at[n], sems_in.at[n])

    def store(n):
        start = pl.multiple_of((place[0] ^ (n + 1)) * count + first, 128)
        return pltpu.make_async_copy(wide.at[n], out_hbm.at[:, pl.ds(start, width)], sems_out.at[n])

    for n in range(GROUP - 1):
        fetch(n).start()
    for n in range(GROUP - 1):
        fetch(n).wait()
        wide[n] = got[n].astype(F32)
        store(n).start()
    for n in range(GROUP - 1):
        store(n).wait()


def place_call(first, place, arrived, out):
    rows, width = arrived[0].shape
    return pl.pallas_call(
        functools.partial(place_kernel, first),
        out_shape=jax.ShapeDtypeStruct(out.shape, F32),
        in_specs=[SMEM] + anywhere(GROUP),
        out_specs=anywhere(1)[0],
        scratch_shapes=[
            pltpu.VMEM((GROUP - 1, rows, width), BF16), pltpu.VMEM((GROUP - 1, rows, width), F32),
            DMA((GROUP - 1,)), DMA((GROUP - 1,)),
        ],
        input_output_aliases={GROUP: 0},
        cost_estimate=pl.CostEstimate(flops=0, bytes_accessed=18 * rows * width, transcendentals=0),
        compiler_params=params(LIMIT),
        name="place",
    )(place, *arrived, out)


def finish_kernel(t, place, both_ref, denom_ref, pairs_ref, stud_ref, *refs):
    terms, (grad_ref, loss_ref, unit) = refs[:GROUP], refs[GROUP:]
    total = (terms[0][...] + terms[1][...]) + (terms[2][...] + terms[3][...])
    share = grad_ref.shape[0]
    x = stud_ref[...].astype(F32).T
    norm = jnp.sqrt(jnp.sum(x * x, axis=0, keepdims=True) + eps)
    unit[...] = x / norm
    part = unit[pl.ds(pl.multiple_of(place[2] * share, share), share), :]
    along, cross = total[share : share + 1, :], total[share + 1 : share + 2, :]
    grad_ref[...] = (total[:share, :] - part * along) / norm
    sums = both_ref[:, :t]
    mass = pick(to_column(1.0 / (sums * float(t)) * sums * float(t)), pairs_ref[...])
    loss_ref[...] = jnp.log(denom_ref[...]) * mass - cross


def finish_call(t, place, both, denom, pairs, stud, terms, share):
    s, d = stud.shape
    return pl.pallas_call(
        functools.partial(finish_kernel, t),
        out_shape=(jax.ShapeDtypeStruct((share, s), F32), jax.ShapeDtypeStruct((1, s), F32)),
        in_specs=[SMEM] + vmem(4 + GROUP),
        out_specs=tuple(vmem(2)),
        scratch_shapes=[pltpu.VMEM((d, s), F32)],
        compiler_params=params(8),
        name="finish",
    )(place, both, denom, pairs, stud, *terms)


def body(teacher_features, student_features, v, pairing):
    n_rows, n_proto = lax.axis_size("rows"), lax.axis_size("proto")
    r, p = lax.axis_index("rows"), lax.axis_index("proto")
    d, local_k = v.shape
    total_k = local_k * n_proto
    kl = local_k // GROUP
    t_dev, s_dev = teacher_features.shape[0], student_features.shape[0]
    t, s = t_dev * n_rows, s_dev * n_rows
    at, group = r % GROUP, r // GROUP
    top = (p * 2) // n_proto
    place = jnp.stack([at, group, p, top]).astype(jnp.int32)
    factor = total_k / 64.0 / student_temp

    def swap_rows(x, n):
        return lax.ppermute(x, "rows", [(j, j ^ n) for j in range(n_rows)])

    def swap_proto(x, n):
        return lax.ppermute(x, "proto", [(j, j ^ n) for j in range(n_proto)])

    def over(swap, size, x):
        n = 1
        while n < size:
            x = (x + swap(x, n)) + (swap(x, 2 * n) + swap(x, 3 * n))
            n *= 4
        return x

    def over_proto(x):
        return over(swap_proto, n_proto, x)

    def over_group(x):
        return over(swap_rows, GROUP, x)

    def total(x):
        return over_group(over_proto(x))

    def join(x, n, other=None):
        other = swap_rows(x, n) if other is None else other
        low = (r // n) % 2 == 0
        return jnp.concatenate([jnp.where(low, x, other), jnp.where(low, other, x)], axis=0)

    own_pairs = pairing.reshape(1, s_dev)
    unit, inv = unit_call(place, v, kl)
    packed = prepare_call(teacher_features, student_features, own_pairs)
    blocks = [packed] + [swap_rows(packed, n) for n in range(1, GROUP)]
    blocks[-1], unit, inv = lax.optimization_barrier((blocks[-1], unit, inv))
    for n in (1, 2):
        low = (at // n) % 2 == 0
        blocks = [jnp.where(low, blocks[j], blocks[j ^ n]) for j in range(GROUP)]
    packed = jnp.stack(blocks)
    teach_all, near = packed[:, :t_dev], packed[:, t_dev:]

    def pairs_of(rest):
        digits = rest[:, s_dev : s_dev + 2, :s_dev].astype(F32)
        return (digits[:, 0] * 64.0 + digits[:, 1]).astype(jnp.int32).reshape(1, -1)

    near_pairs = pairs_of(near)
    n = GROUP
    while n < n_rows:
        other = swap_rows(teach_all, n)
        teach_all = join(teach_all, n, other)
        n *= 2
    far = swap_rows(lax.optimization_barrier((near, other))[0], GROUP)
    n = 2 * GROUP
    while n < n_rows:
        far = jnp.concatenate([far, swap_rows(jnp.concatenate([near, far], axis=0), n)], axis=0)
        n *= 2
    energy, sums = energy_call(teach_all.reshape(t, d), unit, total_k)
    sums = over_proto(sums)
    near = lax.optimization_barrier((near, sums))[0]
    expo_near, denom_near, near_t, weight, pull = student_call(near, near_pairs, unit, t, True)
    sums = lax.optimization_barrier((over_group(sums), denom_near))[0]
    far_pairs = pairs_of(far)
    expo_far, denom_far, far_t, more_weight = student_call(far, far_pairs, unit, t, False)
    pairs = jnp.concatenate([near_pairs, far_pairs], axis=1)
    (sums,) = iterate_call(sums, energy, total_k)
    sums = lax.optimization_barrier((sums, far))[0]
    both, scaled = iterate_call(total(sums), energy, total_k, (denom_near, denom_far))
    mean = mean_call(near_pairs, unit, scaled)
    both = total(both)
    students = (expo_near, expo_far, near_t, far_t, weight, more_weight)

    rows = d // n_rows
    width = kl // (CHUNKS * SPLIT)
    offsets = [sum(SIZES[:n]) for n in range(len(SIZES))]
    more = (pull, mean)
    pieces = []
    for first, chunks in zip(offsets, SIZES):
        out = head_call(
            first, chunks, place, both, pairs, students, inv, scaled, v, factor, rows, more
        )
        if first == 0:
            body_rows, send, tail = out[GROUP:]
        more = (out[0],)
        arrived = []
        for n in range(1, GROUP):
            share = out[n]
            if pieces and n == GROUP - 1:
                share = lax.optimization_barrier((share, pieces[-1]))[0]
            arrived.append(swap_rows(share, n))
        pieces.append(arrived)
    proto_grad = out[0]
    for part, arrived in enumerate(pieces[:-1]):
        proto_grad = place_call(offsets[part] * width, place, arrived, proto_grad)
    n = n_proto // 2
    while n >= 1:
        if n < n_proto // 2:
            height = body_rows.shape[0] // 2
            bit = (p // n) % 2
            send = lax.dynamic_slice_in_dim(body_rows, (1 - bit) * height, height, 0)
            body_rows = lax.dynamic_slice_in_dim(body_rows, bit * height, height, 0)
            send = jnp.concatenate([send, tail], axis=0)
        got = lax.optimization_barrier((swap_proto(send, n), out[1] if n == n_proto // 2 else proto_grad))[0]
        height = body_rows.shape[0]
        body_rows, tail = body_rows + got[:height], tail + got[height:]
        n //= 2
    terms = jnp.concatenate([body_rows, tail], axis=0)

    def block(n):
        return lax.dynamic_slice_in_dim(terms, (at ^ n) * s_dev, s_dev, 1)

    parts = [block(0)] + [swap_rows(block(n), n) for n in range(1, GROUP)]
    proto_grad = place_call(offsets[-1] * width, place, pieces[-1], proto_grad)
    own = lax.dynamic_slice_in_dim(both, t + at * s_dev, s_dev, 1)
    student_grad, loss = finish_call(t, place, both, own, own_pairs, student_features, parts, d // n_proto)
    return (proto_grad, student_grad.T, loss.reshape(s_dev))


def solution(mesh):
    return jax.shard_map(
        body,
        mesh=mesh,
        in_specs=(P("rows", None), P("rows", None), P(None, "proto"), P("rows")),
        out_specs=(P("rows", "proto"), P("rows", "proto"), P("rows")),
        check_vma=False,
    )
```
